32 devices in a mesh: ifg: 16 (over z, y, x), tile: 2 (over core).
Axes of the slice: x: 2, y: 2, z: 4, core: 2. Of those that a mesh axis runs over, the one named last changes fastest.
Arguments:
- phases: float32 [1024, 128, 64], P('ifg', 'tile'), may hold values from -6 to 6
- pairs: int32 [1024, 2], replicated, may hold values from 0 to 299, as said below
- class_weights: float32 [8, 1024], replicated, may hold values from 0.05 to 1
- classes: int32 [128, 64], P('tile', 'ifg'), may hold values from 0 to 7
Outputs:
- corrected: float32 [128, 64, 300], P('tile', 'ifg')
The draws below stay inside these ranges and needn't reach their ends.
Inputs may be any that keep to these rules, and one draw needn't show every extreme that they name: pairs[i,0] < pairs[i,1] <= pairs[i,0] + 8; some interferogram starts at date 0 and some ends at date 300 - 1.
All inputs are finite; a program needn't handle non-finite values.
Results may differ from the reference program's by a relative error of at most 0.0003.
Values sent between devices are 32-bit elements; how exact they have to be, the bound alone decides.
A program may use at most 128 MiB of HBM per device.

```python
import math
import jax
import jax.numpy as jnp
from jax import lax

DATES = 300
NIFG = 1024
CLASSES = 8
MAXGAP = 8
R = 3
ROWS = 128
COLS = 64


def draw_pairs(key, part):
    first_key, second_key = jax.random.split(jax.random.fold_in(key, 17))
    first = jax.random.randint(first_key, (NIFG,), 0, DATES - 1)
    first = first.at[0].set(0).at[NIFG - 1].set(DATES - 2)
    spacing = jax.random.randint(second_key, (NIFG,), 1, MAXGAP + 1)
    second = jnp.minimum(first + spacing, DATES - 1)
    return jnp.stack([first, second], axis=1).astype(jnp.int32)


def plant(values, own_key, least, high):
    extent = values.shape
    index_at = [jax.random.randint(jax.random.fold_in(own_key, axis), (), 0, extent[axis]) for axis in range(len(extent))]
    values = values.at[tuple(index_at)].set(least)
    longest = extent.index(max(extent))
    index_at[longest] = (index_at[longest] + 1) % extent[longest]
    return values.at[tuple(index_at)].set(high)


def steps_of(stream_key, extent, pieces, least, high):
    gain, own = 1.0, jax.random.fold_in(stream_key, 6)
    for axis_at, parts in pieces:
        steps = jnp.exp(jax.random.uniform(jax.random.fold_in(own, axis_at), (parts,), jnp.float32, least / len(pieces), high / len(pieces)))
        gain = gain * jnp.repeat(steps, extent[axis_at] // parts).reshape([-1 if axis == axis_at else 1 for axis in range(len(extent))])
    return gain


def noise(own_key, shape, deviation, reach, cuts=(), held_as=jnp.bfloat16):
    entries = jax.random.normal(own_key, shape, jnp.float32) * deviation
    if len(cuts) > 0:
        entries = steps_of(own_key, shape, cuts, -0.22, 0.18) * entries
    return jnp.clip(entries, min=-reach, max=reach).astype(held_as)


def setup_inputs(seed: int = 0) -> dict:
    key_of = jax.random.split(jax.random.key(seed), 5)
    phases = noise(key_of[0], (NIFG, ROWS, COLS), 1.0, 6.0, ((0, 16), (1, 2)), jnp.float32)
    pairs = draw_pairs(jax.random.fold_in(key_of[4], 71), 0)
    class_weights = jnp.clip(jnp.exp(jax.random.uniform(key_of[2], (CLASSES, NIFG), jnp.float32, math.log(0.05), math.log(1.0))), 0.05, 1.0)
    classes = plant(jax.random.randint(key_of[3], (ROWS, COLS), 0, CLASSES), jax.random.fold_in(key_of[3], 1), 0, CLASSES - 1).astype(jnp.int32)
    return dict(phases=phases, pairs=pairs, class_weights=class_weights, classes=classes)


smooth_weight = 1.0
anchor_weight = 0.1

def incidence_matrix(pairs):
    dates = jnp.arange(DATES, dtype=jnp.int32)[:, None]
    plus = (dates == pairs[:, 1][None, :]).astype(jnp.float32)
    minus = (dates == pairs[:, 0][None, :]).astype(jnp.float32)
    return plus - minus

def prior_matrix():
    second = jnp.arange(DATES - 2, dtype=jnp.int32)[:, None]
    columns = jnp.arange(DATES, dtype=jnp.int32)[None, :]
    diffs = (columns == second).astype(jnp.float32) - 2.0 * (columns == second + 1).astype(jnp.float32) + (columns == second + 2).astype(jnp.float32)
    curvature = jnp.dot(diffs.T.astype(jnp.float32), diffs.astype(jnp.float32), precision=lax.Precision.HIGHEST, preferred_element_type=jnp.float32)
    return smooth_weight * curvature + anchor_weight * jnp.eye(DATES, dtype=jnp.float32)

def invert(matrix):
    factor = jnp.linalg.cholesky(matrix)
    return jax.scipy.linalg.cho_solve((factor, True), jnp.eye(DATES, dtype=jnp.float32))

def filter_taps():
    offsets = jnp.arange(-R, R + 1).astype(jnp.float32)
    values = jnp.exp(-offsets * offsets / 4.5)
    return values / jnp.sum(values)

def reference(phases, pairs, class_weights, classes):
    incidence = incidence_matrix(pairs)
    normal = jnp.einsum('di,ki,ei->kde', incidence, class_weights, incidence, precision=lax.Precision.HIGHEST)
    inverse = jax.vmap(invert)(normal + prior_matrix()[None])

    def invert_row(row_index):
        phase_row = lax.dynamic_slice_in_dim(phases, row_index, 1, 1)[:, 0, :]
        class_row = lax.dynamic_slice_in_dim(classes, row_index, 1, 0)[0]
        onehot = (class_row[None, :] == jnp.arange(CLASSES, dtype=jnp.int32)[:, None]).astype(jnp.float32)
        pixel_weights = jnp.dot(class_weights.T.astype(jnp.float32), onehot.astype(jnp.float32), precision=lax.Precision.HIGHEST, preferred_element_type=jnp.float32)
        right_terms = jnp.einsum('ip,di->pd', pixel_weights * phase_row, incidence, precision=lax.Precision.HIGHEST)
        result = jnp.zeros((COLS, DATES), jnp.float32)
        for member in range(CLASSES):
            solved = jnp.einsum('pd,ed->pe', right_terms, inverse[member], precision=lax.Precision.HIGHEST)
            result = result + onehot[member][:, None] * solved
        return result
    displacement = lax.map(invert_row, jnp.arange(ROWS, dtype=jnp.int32))
    filter_weights = filter_taps()
    padded = jnp.pad(displacement, ((R, R), (R, R), (0, 0)))
    across = filter_weights[0] * padded[:, 0:COLS]
    for offset in range(1, 2 * R + 1):
        across = across + filter_weights[offset] * padded[:, offset:offset + COLS]
    atmosphere = filter_weights[0] * across[0:ROWS]
    for offset in range(1, 2 * R + 1):
        atmosphere = atmosphere + filter_weights[offset] * across[offset:offset + ROWS]
    return displacement - atmosphere
```

```python
import functools
import math
import jax
import jax.numpy as jnp
from jax import lax
from jax.experimental import pallas as pl
from jax.experimental.pallas import tpu as pltpu
from jax.sharding import PartitionSpec as P

DATES = 300
CLASSES = 8
MAXGAP = 8
R = 3
LANES = 128
HALF = DATES // 2
MEET = HALF - MAXGAP // 2
LAST = MEET + MAXGAP
ROWS = -(-LAST // 16) * 16
OUT = -(-HALF // 8) * 8
CUT = (OUT // 16) * 8
BLOCKS = MEET // 8
PARTS = ((1, 2), (0, 3))
MESH = pl.DeviceIdType.MESH

smooth_weight = 1.0
anchor_weight = 0.1

NORM = sum(math.exp(-j * j / 4.5) for j in range(-R, R + 1))
F32, BF16 = jnp.float32, jnp.bfloat16


def split3(value):
    high = value.astype(BF16)
    rest = value - high.astype(F32)
    middle = rest.astype(BF16)
    low = (rest - middle.astype(F32)).astype(BF16)
    return (high, middle, low)


def split2(value):
    high = value.astype(BF16)
    return high, (value - high.astype(F32)).astype(BF16)


def dot_nt(a, b):
    return lax.dot_general(a, b, (((1,), (1,)), ((), ())), preferred_element_type=F32)


def dot_nn(a, b):
    return lax.dot_general(a, b, (((1,), (0,)), ((), ())), preferred_element_type=F32)


def iota(shape, dim):
    return lax.broadcasted_iota(jnp.int32, shape, dim)


def one(cond):
    return jnp.where(cond, 1.0, 0.0)


def tap(delta):
    near = jnp.exp((delta * delta).astype(F32) * (-1.0 / 4.5)) * (1.0 / NORM)
    return jnp.where(jnp.abs(delta) <= R, near, 0.0)


def tap_at(delta):
    return math.exp(-delta * delta / 4.5) / NORM if abs(delta) <= R else 0.0


def swap(value):
    return pltpu.roll(value, LANES // 2, 1)


def bands(pairs_ref, w_ref, band):
    nifg = pairs_ref.shape[1]
    first, second = pairs_ref[0:1, :], pairs_ref[1:2, :]
    gap = second - first
    row = iota((ROWS, nifg), 0)
    left = [one(row == first), one(row == second), one(DATES - 1 - row == second), one(DATES - 1 - row == first)]
    left = jnp.concatenate(left, axis=0).astype(BF16)
    w = w_ref[...]
    zero = jnp.zeros((CLASSES, nifg), F32)
    grouped = [jnp.where(gap == g, w, 0.0) for g in range(1, MAXGAP + 1)] + [w] + [zero] * 7
    high, middle, low = split3(jnp.concatenate(grouped, axis=0))
    both = dot_nt(left, jnp.concatenate([high, middle], axis=0))
    total = both[:, :LANES] + (both[:, LANES:] + dot_nt(left, low))
    ff, fs, bs, bf = [total[i * ROWS:(i + 1) * ROWS] for i in range(4)]
    lane = iota((ROWS, LANES), 1)
    t = iota((ROWS, LANES), 0)
    front, used = lane < LANES // 2, (lane & (LANES // 2 - 1)) < CLASSES
    band[0] = jnp.where(used, jnp.where(front, swap(ff + fs), bs + bf), 0.0) + (
        smooth_weight * (1.0 + 4.0 * one(t >= 1) + one(t >= 2)) + anchor_weight)
    off = jnp.where(front, ff, swap(bs))
    for g in range(1, MAXGAP + 1):
        here = off if g == 1 else pltpu.roll(off, LANES - 8 * (g - 1), 1)
        here = -jnp.where(used, here, 0.0)
        if g == 1:
            here += smooth_weight * (-2.0 - 2.0 * one(t >= 1))
        elif g == 2:
            here += smooth_weight
        band[g] = jnp.where(t + g < LAST, here, 0.0)


def factor(band, low):
    zero = jnp.zeros((1, LANES), F32)
    keys = [(j, h) for j in range(MAXGAP) for h in range(MAXGAP - j)]

    def step(at, acc):
        c = [band[h, at, :] for h in range(MAXGAP + 1)]
        c = [c[h] - acc[(0, h)] for h in range(MAXGAP)] + [c[MAXGAP]]
        inv = 1.0 / c[0]
        low[0, at, :] = inv
        fresh = {}
        for j in range(1, MAXGAP + 1):
            lj = c[j] * inv
            low[j, at, :] = lj
            for h in range(MAXGAP - j + 1):
                term = lj * c[j + h]
                old = acc.get((j, h))
                fresh[(j - 1, h)] = term if old is None else old + term
        return fresh

    def block(b, carry):
        acc = dict(zip(keys, carry))
        base = pl.multiple_of(b * 8, 8)
        for s in range(8):
            acc = step(pl.ds(base + s, 1), acc)
        return tuple(acc[k] for k in keys)

    acc = dict(zip(keys, lax.fori_loop(0, BLOCKS, block, tuple(zero for _ in keys))))
    for t in range(8 * BLOCKS, MEET):
        acc = step(pl.ds(t, 1), acc)
    acc = {(j, h): acc[(j, h)] + swap(acc[(MAXGAP - 1 - j - h, h)]) for j, h in keys}
    for t in range(MEET, LAST):
        acc = step(pl.ds(t, 1), acc)


def prepare(pairs_ref, w_ref, cls_ref, per, count, inc_ref, wpx_ref, lpx_ref, band, low):
    nifg = pairs_ref.shape[1]
    half = nifg // 2
    q, lane = iota((LANES, LANES), 0), iota((LANES, LANES), 1)
    local = q & 63
    place = (local < 3 * CLASSES) & ((q >= 64) == (lane >= 64))
    classes = cls_ref[...]
    classes = jnp.concatenate([classes, classes], axis=1)
    onehot = [one(place & ((local & 7) == classes[c:c + 1, :])) for c in range(4)]
    onehot = jnp.concatenate(onehot, axis=1).astype(BF16)

    parts = [p.astype(F32) for p in split3(w_ref[...])]
    ends = [jnp.broadcast_to(pairs_ref[i:i + 1, :].astype(F32), (8, nifg)) for i in range(2)]
    stack = jnp.concatenate(parts + ends + [jnp.zeros((24, nifg), F32)], axis=0)
    by_ifg = jnp.concatenate([stack, stack], axis=0).T.reshape(count, 2 * per, LANES)
    ours, theirs = by_ifg[:, :per].reshape(half, LANES), by_ifg[:, per:].reshape(half, LANES)
    packed = jnp.where(iota((half, LANES), 1) < 64, ours, theirs)
    weights = dot_nn(packed.astype(BF16), onehot)
    for c in range(4):
        wpx_ref[c] = weights[:, c * LANES:(c + 1) * LANES]
    ends = packed.T
    row = iota((ROWS, half), 0)
    inside = row < HALF
    row = row.astype(F32)
    for h in range(2):
        first, second = ends[64 * h + 24:64 * h + 25, :], ends[64 * h + 32:64 * h + 33, :]
        front = one(inside & (row == second)) - one(inside & (row == first))
        back = one(inside & (DATES - 1.0 - row == second)) - one(inside & (DATES - 1.0 - row == first))
        inc_ref[h, 0:ROWS, :] = front.astype(BF16)
        inc_ref[h, ROWS:, :] = back.astype(BF16)

    bands(pairs_ref, w_ref, band)
    factor(band, low)
    used = (iota((ROWS, LANES), 1) & 63) < CLASSES
    valid = iota((ROWS, LANES), 0) < LAST
    for g in range(MAXGAP + 1):
        high, middle, rest = [p.astype(F32) for p in split3(jnp.where(used & valid, low[g], 0.0))]
        value = high + pltpu.roll(middle, 8, 1) + pltpu.roll(rest, 16, 1)
        each = dot_nn(value.astype(BF16), onehot)
        for p, columns in enumerate(PARTS):
            for i, c in enumerate(columns):
                lpx_ref[p, g, pl.ds(i, ROWS, stride=2), :] = each[:, c * LANES:(c + 1) * LANES]


def fill_filters(dirs, has_left, has_right, k_ref, sel_ref, tile_ref):
    shape = (2 * 256, LANES)
    row, lane = iota(shape, 0), iota(shape, 1)
    out_c, out_r = row & 3, (row & 255) >> 2
    match = (row >= 256) == (lane >= 64)
    delta = out_r - (lane & 63)
    vertical = jnp.where(match, tap(delta), 0.0)
    straight = one(match & (delta == 0))

    def column(at, has):
        taps = [tap_at(c - at) for c in range(4)]
        near = jnp.where(out_c == 0, taps[0], jnp.where(out_c == 1, taps[1], jnp.where(out_c == 2, taps[2], taps[3])))
        value = -vertical * near
        if 0 <= at < 4:
            value += jnp.where(out_c == at, straight, 0.0)
        return value if has is None else value * has

    sets = [(1, None, 2, None), (-3, has_left, -2, has_left), (5, has_right, 6, has_right), (0, None, 3, None), (-1, has_left, 4, has_right)]
    for i, (a, has_a, b, has_b) in enumerate(sets):
        high, middle = split2(jnp.concatenate([column(a, has_a), column(b, has_b)], axis=1))
        k_ref[i, 0] = high
        k_ref[i, 1] = middle
    for d, (_, _, sent, _) in enumerate(dirs):
        shape = (16, 2 * LANES)
        row, lane = iota(shape, 0), iota(shape, 1)
        pick = ((row >> 2) == (lane >> 6)) & ((row & 3) < R) & ((lane & 63) == sent + (row & 3))
        sel_ref[d] = one(pick).astype(BF16)
    for p, columns in enumerate(PARTS):
        for d, (_, has, _, got) in enumerate(dirs):
            shape = (2 * 256, 48)
            row, lane = iota(shape, 0), iota(shape, 1)
            side, slot = lane >> 4, lane & 15
            col = jnp.where((slot >> 3) == 0, columns[0], columns[1]) + 4 * (side - 1)
            out_c, out_r = row & 3, (row & 255) >> 2
            ok = ((slot & 3) < R) & (((slot >> 2) & 1) == (row >> 8))
            value = jnp.where(ok, -tap(out_r - got - (slot & 3)) * tap(out_c - col), 0.0)
            there = jnp.where(side == 0, has_left, jnp.where(side == 2, has_right, 1.0))
            value = value * there if has is None else value * there * one(has)
            high, middle = split2(value)
            tile_ref[p, d, 0] = high
            tile_ref[p, d, 1] = middle


def kernel(tile_rows, tiles, phases_ref, pairs_ref, w_ref, cls_ref, out_ref,
           phase, blocks, recv, inc_ref, wpx_ref, lpx_ref, band, low, k_ref, sel_ref, tile_ref,
           z_ref, y_ref, x_ref, edge, halo_one, halo_two, halo_tile, acc,
           load_sem, own_sem, all_send, all_recv, send_sem, recv_sem):
    me, core = lax.axis_index("ifg"), lax.axis_index("tile")
    count = lax.axis_size("ifg")
    own = phase.shape[0]
    per = own // 2
    cols = phase.shape[2]
    left, right = lax.rem(me + count - 1, count), lax.rem(me + 1, count)
    has_left, has_right = me > 0, me < count - 1
    if tiles == 2:
        dirs = [(1 - core, None, jnp.where(core == 0, tile_rows - R, 0), jnp.where(core == 0, tile_rows, -R))]
    else:
        dirs = [(lax.rem(core + tiles - 1, tiles), core > 0, 0, -R),
                (lax.rem(core + 1, tiles), core < tiles - 1, tile_rows - R, tile_rows)]

    pieces = 2
    loads = []
    for i in range(pieces):
        for h in range(2):
            span = pl.ds(h * per + i * (per // pieces), per // pieces)
            loads.append(pltpu.make_async_copy(phases_ref.at[span], phase.at[span], load_sem.at[2 * i + h]))
            loads[-1].start()

    barrier = pltpu.get_barrier_semaphore()

    def greet(k, _):
        pl.semaphore_signal(barrier, inc=1, device_id=(lax.rem(me + k, count), core), device_id_type=MESH)
        return _

    lax.fori_loop(1, count, greet, 0)
    near = [[(me, tile), (left, tile), (right, tile)] for tile, _, _, _ in dirs]
    for group in near:
        for partner in group:
            pl.semaphore_signal(barrier, inc=1, device_id=partner, device_id_type=MESH)

    for i in range(pieces):
        loads[2 * i].wait()
        loads[2 * i + 1].wait()

        def turn(q, _):
            value = jnp.concatenate([phase[q], phase[q + per]], axis=0).T
            blocks[pl.ds(q, cols, stride=per), :] = value
            return _

        lax.fori_loop(i * (per // pieces), (i + 1) * (per // pieces), turn, 0, unroll=4)
    pl.semaphore_wait(barrier, count - 1 + 3 * len(dirs))

    spans = [(per, 2 * per), (0, per), (3 * per, per)]

    def exchange(i, k, src):
        peer = lax.rem(me + k, count)
        at, size = spans[i]
        return pltpu.make_async_remote_copy(
            src_ref=blocks.at[pl.ds(pl.multiple_of(peer * 4 * per + at, 8), size)], dst_ref=recv.at[src, pl.ds(at, size)],
            send_sem=all_send.at[i, k], recv_sem=all_recv.at[i, k], device_id=(peer, core), device_id_type=MESH)

    for group in ((0,), (1, 2)):
        def send_blocks(k, _, group=group):
            for i in group:
                exchange(i, k, me).start()
            return _

        lax.fori_loop(1, count, send_blocks, 0)
    mine = pltpu.make_async_copy(blocks.at[pl.ds(pl.multiple_of(me * 4 * per, 8), 4 * per)], recv.at[me], own_sem)
    mine.start()

    def absent(cond, *refs):
        @pl.when(jnp.logical_not(cond))
        def _():
            for ref in refs:
                ref[...] = jnp.zeros(ref.shape, F32)

    absent(has_left, halo_one.at[0], halo_two.at[0])
    absent(has_right, halo_one.at[1], halo_two.at[1])
    for p in range(2):
        for d, (_, has, _, _) in enumerate(dirs):
            absent(has_left if has is None else has_left & has, halo_tile.at[p, d, 0])
            absent(has_right if has is None else has_right & has, halo_tile.at[p, d, 2])
            if has is not None:
                absent(has, halo_tile.at[p, d, 1])

    prepare(pairs_ref, w_ref, cls_ref, per, count, inc_ref, wpx_ref, lpx_ref, band, low)
    fill_filters(dirs, one(has_left), one(has_right), k_ref, sel_ref, tile_ref)
    mine.wait()

    def take(group):
        def take_blocks(k, _):
            for i in group:
                exchange(i, k, lax.rem(me + count - k, count)).wait_recv()
            return _

        lax.fori_loop(1, count, take_blocks, 0)

    low_lanes = iota((ROWS, LANES), 1) < LANES // 2

    def right_side(p):
        values = []
        for c in PARTS[p]:
            got = recv[:, c * per:(c + 1) * per, :].reshape(count * per, LANES)
            values.append(got * wpx_ref[c])
        high, middle = split2(jnp.concatenate(values, axis=1))
        a, b = [dot_nn(inc_ref[h], high) + dot_nn(inc_ref[h], middle) for h in range(2)]
        for i in range(2):
            at = slice(i * LANES, (i + 1) * LANES)
            aa, ab, ba, bb = a[:ROWS, at], a[ROWS:, at], b[:ROWS, at], b[ROWS:, at]
            z_ref[pl.ds(i, ROWS, stride=2), :] = jnp.where(low_lanes, aa, bb) + swap(jnp.where(low_lanes, ab, ba))

    def forward(p):
        def step(t, a):
            at = pl.ds(t, 2)
            y = a[0]
            y_ref[at, :] = y * lpx_ref[p, 0, at, :]
            return [v - lpx_ref[p, j + 1, at, :] * y for j, v in enumerate(a[1:])]

        def block(b, carry):
            a = list(carry)
            base = pl.multiple_of(b * 16, 16)
            for s in range(8):
                a = step(base + 2 * s, a + [z_ref[pl.ds(base + 2 * s + 16, 2), :]])
            return tuple(a)

        a = list(lax.fori_loop(0, BLOCKS, block, tuple(z_ref[2 * t:2 * t + 2, :] for t in range(8))))
        for t in range(8 * BLOCKS, MEET):
            a = step(2 * t, a + [z_ref[2 * t + 16:2 * t + 18, :]])
        a = [a[j] + swap(a[7 - j]) for j in range(8)]
        for t in range(MEET, LAST):
            a = step(2 * t, a)

    def backward(p, send):
        one_ref, two_ref = x_ref.at[PARTS[p][0]], x_ref.at[PARTS[p][1]]

        def step(t, later, keep=True):
            at = pl.ds(2 * t, 2)
            value = y_ref[at, :]
            for g in range(len(later), 0, -1):
                value = value - lpx_ref[p, g, at, :] * later[g - 1]
            if keep:
                one_ref[pl.ds(t, 1), :] = value[0:1]
                two_ref[pl.ds(t, 1), :] = value[1:2]
            return [value] + later[:7]

        later = []
        for t in range(LAST - 1, 8 * BLOCKS - 1, -1):
            later = step(t, later, t < OUT)

        def block(b, carry):
            later = list(carry)
            base = pl.multiple_of(b * 8, 8)
            for s in range(7, -1, -1):
                later = step(base + s, later)
            return tuple(later)

        cut = CUT // 8
        carry = lax.fori_loop(0, BLOCKS - cut, lambda n, c: block(BLOCKS - 1 - n, c), tuple(later))
        send(0, pl.ds(CUT, OUT - CUT))
        lax.fori_loop(0, cut, lambda n, c: block(cut - 1 - n, c), carry)
        send(1, pl.ds(0, CUT))

    def copy(i, src, dst, device):
        return pltpu.make_async_remote_copy(src_ref=src, dst_ref=dst, send_sem=send_sem.at[i],
                                            recv_sem=recv_sem.at[i], device_id=device, device_id_type=MESH)

    sides = [[], []]

    def send_one(piece, span):
        src = x_ref.at[pl.ds(1, 2), span]
        sides[0].append(copy(2 * piece, src, halo_one.at[1, :, span], (left, core)))
        sides[1].append(copy(2 * piece + 1, src, halo_one.at[0, :, span], (right, core)))
        pl.when(has_left)(sides[0][-1].start)
        pl.when(has_right)(sides[1][-1].start)

    def send_two(piece, span):
        sides[0].append(copy(4 + 2 * piece, x_ref.at[0, span], halo_two.at[1, span], (left, core)))
        sides[1].append(copy(5 + 2 * piece, x_ref.at[3, span], halo_two.at[0, span], (right, core)))
        pl.when(has_left)(sides[0][-1].start)
        pl.when(has_right)(sides[1][-1].start)

    edges = []

    def both(a, b):
        return b if a is None else a if b is None else a & b

    def when(cond, action):
        action() if cond is None else pl.when(cond)(action)

    def solved(p):
        value = jnp.concatenate([x_ref[c] for c in PARTS[p]], axis=1)
        return split3(value)

    def send_edges(p, parts):
        for d, (_, has, _, _) in enumerate(dirs):
            edge[p, d] = dot_nt(sel_ref[d], parts[0]) + (dot_nt(sel_ref[d], parts[1]) + dot_nt(sel_ref[d], parts[2]))
            opposite = len(dirs) - 1 - d
            got = dirs[opposite][1]
            for i, (slot, to, came) in enumerate(((1, None, None), (2, has_left, has_right), (0, has_right, has_left))):
                c = copy(8 + (p * len(dirs) + d) * 3 + i, edge.at[p, d], halo_tile.at[p, opposite, slot], near[d][i])
                edges.append((c, both(has, to), both(got, came)))
                when(edges[-1][1], c.start)

    def apply(i, parts):
        return dot_nt(k_ref[i, 0], parts[0]) + (dot_nt(k_ref[i, 0], parts[1]) + dot_nt(k_ref[i, 1], parts[0]))

    def apply_tile(p):
        total = None
        for d in range(len(dirs)):
            high, middle = split2(halo_tile[p, d].reshape(48, OUT))
            term = dot_nn(tile_ref[p, d, 0], high) + (dot_nn(tile_ref[p, d, 0], middle) + dot_nn(tile_ref[p, d, 1], high))
            total = term if total is None else total + term
        return total

    def wait_sides(first):
        for i in (2 * first, 2 * first + 1):
            pl.when(has_right)(sides[0][i].wait_recv)
            pl.when(has_left)(sides[1][i].wait_recv)

    take((0,))
    right_side(0)
    forward(0)
    backward(0, send_one)
    parts = solved(0)
    send_edges(0, parts)
    acc[...] = apply(0, parts)

    take((1, 2))
    right_side(1)
    forward(1)
    backward(1, send_two)
    parts = solved(1)
    send_edges(1, parts)
    wait_sides(0)
    for c, _, came in edges[:3 * len(dirs)]:
        when(came, c.wait_recv)
    total = acc[...] + apply(3, parts)
    for side in range(2):
        total += apply(1 + side, split2(jnp.concatenate([halo_one[side, 0], halo_one[side, 1]], axis=1)))
    total += apply_tile(0)
    for c, _, came in edges[3 * len(dirs):]:
        when(came, c.wait_recv)
    total += apply_tile(1)
    wait_sides(1)
    total += apply(4, split2(jnp.concatenate([halo_two[0], halo_two[1]], axis=1)))

    front, back = total[:256], split2(total[256:])
    row, lane = iota((OUT, DATES), 0), iota((OUT, DATES), 1)
    turned = one((row < HALF) & (row == DATES - 1 - lane)).astype(BF16)
    later = dot_nn(back[0], turned) + dot_nn(back[1], turned)
    out_ref[...] = later
    out_ref[:, 0:LANES] = front[:, 0:LANES]
    tail = front[:, LANES:OUT]
    out_ref[:, LANES:OUT] = later[:, LANES:OUT] + jnp.where(iota(tail.shape, 1) < HALF - LANES, tail, 0.0)

    def drain(k, _):
        for i in range(3):
            exchange(i, k, me).wait_send()
        return _

    lax.fori_loop(1, count, drain, 0)
    for has, group in ((has_left, sides[0]), (has_right, sides[1])):
        for c in group:
            pl.when(has)(c.wait_send)
    for c, went, _ in edges:
        when(went, c.wait_send)


def on_device(tiles, phases, pairs, class_weights, classes):
    own, tile_rows, cols = phases.shape
    tile_cols = classes.shape[1]
    count = cols // tile_cols
    assert tile_rows == 64 and tile_cols == 4
    if own % 16:
        more = -own % 16
        phases = jnp.pad(phases, ((0, more), (0, 0), (0, 0)))
        pairs = jnp.pad(pairs.reshape(count, own, 2), ((0, 0), (0, more), (0, 0))).reshape(-1, 2)
        class_weights = jnp.pad(class_weights.reshape(CLASSES, count, own), ((0, 0), (0, 0), (0, more))).reshape(CLASSES, -1)
        own += more
    nifg = pairs.shape[0]
    per = own // 2
    dirs = 1 if tiles == 2 else 2
    vmem = pl.BlockSpec(memory_space=pltpu.VMEM)
    copies = 8 + 6 * dirs

    corrected = pl.pallas_call(
        functools.partial(kernel, tile_rows, tiles),
        out_shape=jax.ShapeDtypeStruct((256, DATES), F32),
        in_specs=[pl.BlockSpec(memory_space=pl.ANY)] + [vmem] * 3,
        out_specs=vmem,
        scratch_shapes=[
            pltpu.VMEM((own, tile_rows, cols), F32),
            pltpu.VMEM((cols * per, LANES), F32),
            pltpu.VMEM((count, 4 * per, LANES), F32),
            pltpu.VMEM((2, 2 * ROWS, nifg // 2), BF16),
            pltpu.VMEM((4, nifg // 2, LANES), F32),
            pltpu.VMEM((2, MAXGAP + 1, 2 * ROWS, LANES), F32),
            pltpu.VMEM((MAXGAP + 1, ROWS, LANES), F32),
            pltpu.VMEM((MAXGAP + 1, ROWS, LANES), F32),
            pltpu.VMEM((5, 2, 2 * 256, 2 * LANES), BF16),
            pltpu.VMEM((dirs, 16, 2 * LANES), BF16),
            pltpu.VMEM((2, dirs, 2, 2 * 256, 48), BF16),
            pltpu.VMEM((2 * ROWS, LANES), F32),
            pltpu.VMEM((2 * ROWS, LANES), F32),
            pltpu.VMEM((4, OUT, LANES), F32),
            pltpu.VMEM((2, dirs, 16, OUT), F32),
            pltpu.VMEM((2, 2, OUT, LANES), F32),
            pltpu.VMEM((2, OUT, LANES), F32),
            pltpu.VMEM((2, dirs, 3, 16, OUT), F32),
            pltpu.VMEM((2 * 256, OUT), F32),
            pltpu.SemaphoreType.DMA((4,)),
            pltpu.SemaphoreType.DMA,
            pltpu.SemaphoreType.DMA((3, count)),
            pltpu.SemaphoreType.DMA((3, count)),
            pltpu.SemaphoreType.DMA((copies,)),
            pltpu.SemaphoreType.DMA((copies,)),
        ],
        compiler_params=pltpu.CompilerParams(
            collective_id=0, has_side_effects=True, vmem_limit_bytes=58 * 1024 * 1024
        ),
        name="invert_and_filter",
    )(phases, pairs.T, class_weights, classes.T)
    return corrected.reshape(tile_rows, tile_cols, DATES)


def solution(mesh):
    return jax.shard_map(
        functools.partial(on_device, mesh.shape["tile"]),
        mesh=mesh,
        in_specs=(P("ifg", "tile", None), P(), P(), P("tile", "ifg")),
        out_specs=P("tile", "ifg", None),
        check_vma=False,
    )
```

```python
import functools
import math
import jax
import jax.numpy as jnp
from jax import lax
from jax.experimental import pallas as pl
from jax.experimental.pallas import tpu as pltpu
from jax.sharding import PartitionSpec as P

DATES = 300
CLASSES = 8
MAXGAP = 8
R = 3
LANES = 128
WIDE = 2 * LANES
HALF = DATES // 2
MEET = HALF - MAXGAP // 2
LAST = MEET + MAXGAP
ROWS = -(-LAST // 16) * 16
OUT = -(-HALF // 8) * 8
CUT = (OUT // 16) * 8
BLOCKS = MEET // 8
PARTS = ((1, 2), (0, 3))
MESH = pl.DeviceIdType.MESH

smooth_weight = 1.0
anchor_weight = 0.1

NORM = sum(math.exp(-j * j / 4.5) for j in range(-R, R + 1))
F32, BF16 = jnp.float32, jnp.bfloat16


def split3(value):
    high = value.astype(BF16)
    rest = value - high.astype(F32)
    middle = rest.astype(BF16)
    low = (rest - middle.astype(F32)).astype(BF16)
    return (high, middle, low)


def split2(value):
    high = value.astype(BF16)
    return high, (value - high.astype(F32)).astype(BF16)


def dot_nt(a, b):
    return lax.dot_general(a, b, (((1,), (1,)), ((), ())), preferred_element_type=F32)


def dot_nn(a, b):
    return lax.dot_general(a, b, (((1,), (0,)), ((), ())), preferred_element_type=F32)


def iota(shape, dim):
    return lax.broadcasted_iota(jnp.int32, shape, dim)


def one(cond):
    return jnp.where(cond, 1.0, 0.0)


def tap(delta):
    near = jnp.exp((delta * delta).astype(F32) * (-1.0 / 4.5)) * (1.0 / NORM)
    return jnp.where(jnp.abs(delta) <= R, near, 0.0)


def tap_at(delta):
    return math.exp(-delta * delta / 4.5) / NORM if abs(delta) <= R else 0.0


def swap(value):
    return pltpu.roll(value, LANES // 2, 1)


def bands(pairs_ref, w_ref, band):
    nifg = pairs_ref.shape[1]
    first, second = pairs_ref[0:1, :], pairs_ref[1:2, :]
    gap = second - first
    row = iota((ROWS, nifg), 0)
    left = [one(row == first), one(row == second), one(DATES - 1 - row == second), one(DATES - 1 - row == first)]
    left = jnp.concatenate(left, axis=0).astype(BF16)
    w = w_ref[...]
    zero = jnp.zeros((CLASSES, nifg), F32)
    grouped = [jnp.where(gap == g, w, 0.0) for g in range(1, MAXGAP + 1)] + [w] + [zero] * 7
    high, middle, low = split3(jnp.concatenate(grouped, axis=0))
    both = dot_nt(left, jnp.concatenate([high, middle], axis=0))
    total = both[:, :LANES] + (both[:, LANES:] + dot_nt(left, low))
    ff, fs, bs, bf = [total[i * ROWS:(i + 1) * ROWS] for i in range(4)]
    lane = iota((ROWS, LANES), 1)
    t = iota((ROWS, LANES), 0)
    front, used = lane < LANES // 2, (lane & (LANES // 2 - 1)) < CLASSES
    band[0] = jnp.where(used, jnp.where(front, swap(ff + fs), bs + bf), 0.0) + (
        smooth_weight * (1.0 + 4.0 * one(t >= 1) + one(t >= 2)) + anchor_weight)
    off = jnp.where(front, ff, swap(bs))
    for g in range(1, MAXGAP + 1):
        here = off if g == 1 else pltpu.roll(off, LANES - 8 * (g - 1), 1)
        here = -jnp.where(used, here, 0.0)
        if g == 1:
            here += smooth_weight * (-2.0 - 2.0 * one(t >= 1))
        elif g == 2:
            here += smooth_weight
        band[g] = jnp.where(t + g < LAST, here, 0.0)


def factor(band, low):
    zero = jnp.zeros((1, LANES), F32)
    keys = [(j, h) for j in range(MAXGAP) for h in range(MAXGAP - j)]

    def step(at, acc):
        c = [band[h, at, :] for h in range(MAXGAP + 1)]
        c = [c[h] - acc[(0, h)] for h in range(MAXGAP)] + [c[MAXGAP]]
        inv = 1.0 / c[0]
        low[0, at, :] = inv
        fresh = {}
        for j in range(1, MAXGAP + 1):
            lj = c[j] * inv
            low[j, at, :] = lj
            for h in range(MAXGAP - j + 1):
                term = lj * c[j + h]
                old = acc.get((j, h))
                fresh[(j - 1, h)] = term if old is None else old + term
        return fresh

    def block(b, carry):
        acc = dict(zip(keys, carry))
        base = pl.multiple_of(b * 8, 8)
        for s in range(8):
            acc = step(pl.ds(base + s, 1), acc)
        return tuple(acc[k] for k in keys)

    acc = dict(zip(keys, lax.fori_loop(0, BLOCKS, block, tuple(zero for _ in keys))))
    for t in range(8 * BLOCKS, MEET):
        acc = step(pl.ds(t, 1), acc)
    acc = {(j, h): acc[(j, h)] + swap(acc[(MAXGAP - 1 - j - h, h)]) for j, h in keys}
    for t in range(MEET, LAST):
        acc = step(pl.ds(t, 1), acc)


def prepare(pairs_ref, w_ref, cls_ref, per, count, inc_ref, wpx_ref, lpx_ref, band, low):
    nifg = pairs_ref.shape[1]
    half = nifg // 2
    q, lane = iota((LANES, LANES), 0), iota((LANES, LANES), 1)
    local = q & 63
    place = (local < 3 * CLASSES) & ((q >= 64) == (lane >= 64))
    classes = cls_ref[...]
    classes = jnp.concatenate([classes, classes], axis=1)
    onehot = [one(place & ((local & 7) == classes[c:c + 1, :])) for c in range(4)]
    onehot = jnp.concatenate(onehot, axis=1).astype(BF16)

    parts = [p.astype(F32) for p in split3(w_ref[...])]
    ends = [jnp.broadcast_to(pairs_ref[i:i + 1, :].astype(F32), (8, nifg)) for i in range(2)]
    stack = jnp.concatenate(parts + ends + [jnp.zeros((24, nifg), F32)], axis=0)
    by_ifg = jnp.concatenate([stack, stack], axis=0).T.reshape(count, 2 * per, LANES)
    ours, theirs = by_ifg[:, :per].reshape(half, LANES), by_ifg[:, per:].reshape(half, LANES)
    packed = jnp.where(iota((half, LANES), 1) < 64, ours, theirs)
    weights = dot_nn(packed.astype(BF16), onehot)
    for c in range(4):
        wpx_ref[c] = weights[:, c * LANES:(c + 1) * LANES]
    ends = packed.T
    row = iota((ROWS, half), 0)
    inside = row < HALF
    row = row.astype(F32)
    for h in range(2):
        first, second = ends[64 * h + 24:64 * h + 25, :], ends[64 * h + 32:64 * h + 33, :]
        front = one(inside & (row == second)) - one(inside & (row == first))
        back = one(inside & (DATES - 1.0 - row == second)) - one(inside & (DATES - 1.0 - row == first))
        both = jnp.concatenate([front, back], axis=0).astype(BF16)
        inc_ref[h, :, 0:half] = both
        inc_ref[h, :, half:] = both

    bands(pairs_ref, w_ref, band)
    factor(band, low)
    used = (iota((ROWS, LANES), 1) & 63) < CLASSES
    valid = iota((ROWS, LANES), 0) < LAST
    for g in range(MAXGAP + 1):
        high, middle, rest = [p.astype(F32) for p in split3(jnp.where(used & valid, low[g], 0.0))]
        value = high + pltpu.roll(middle, 8, 1) + pltpu.roll(rest, 16, 1)
        each = dot_nn(value.astype(BF16), onehot)
        for p, columns in enumerate(PARTS):
            for i, c in enumerate(columns):
                lpx_ref[p, g, pl.ds(i, ROWS, stride=2), :] = each[:, c * LANES:(c + 1) * LANES]


def fill_filters(dirs, has_left, has_right, k_ref, sel_ref, tile_ref):
    shape = (2 * 256, LANES)
    row, lane = iota(shape, 0), iota(shape, 1)
    out_c, out_r = row & 3, (row & 255) >> 2
    match = (row >= 256) == (lane >= 64)
    delta = out_r - (lane & 63)
    vertical = jnp.where(match, tap(delta), 0.0)
    straight = one(match & (delta == 0))

    def column(at, has):
        taps = [tap_at(c - at) for c in range(4)]
        near = jnp.where(out_c == 0, taps[0], jnp.where(out_c == 1, taps[1], jnp.where(out_c == 2, taps[2], taps[3])))
        value = -vertical * near
        if 0 <= at < 4:
            value += jnp.where(out_c == at, straight, 0.0)
        return value if has is None else value * has

    sets = [(1, None, 2, None), (0, None, 3, None), (-3, has_left, -2, has_left), (5, has_right, 6, has_right), (-1, has_left, 4, has_right)]
    for i, (a, has_a, b, has_b) in enumerate(sets):
        high, middle = split2(jnp.concatenate([column(a, has_a), column(b, has_b)], axis=1))
        for j, part in enumerate((high, high, middle)):
            k_ref[:, (3 * i + j) * WIDE:(3 * i + j + 1) * WIDE] = part
    for d, (_, _, sent, _) in enumerate(dirs):
        shape = (16, 3 * WIDE)
        row, lane = iota(shape, 0), iota(shape, 1) & (WIDE - 1)
        pick = ((row >> 2) == (lane >> 6)) & ((row & 3) < R) & ((lane & 63) == sent + (row & 3))
        sel_ref[d] = one(pick).astype(BF16)
    for p, columns in enumerate(PARTS):
        for d, (_, has, _, got) in enumerate(dirs):
            shape = (2 * 256, 48)
            row, lane = iota(shape, 0), iota(shape, 1)
            side, slot = lane >> 4, lane & 15
            col = jnp.where((slot >> 3) == 0, columns[0], columns[1]) + 4 * (side - 1)
            out_c, out_r = row & 3, (row & 255) >> 2
            ok = ((slot & 3) < R) & (((slot >> 2) & 1) == (row >> 8))
            value = jnp.where(ok, -tap(out_r - got - (slot & 3)) * tap(out_c - col), 0.0)
            there = jnp.where(side == 0, has_left, jnp.where(side == 2, has_right, 1.0))
            value = value * there if has is None else value * there * one(has)
            high, middle = split2(value)
            for j, part in enumerate((high, high, middle)):
                tile_ref[d, :, (2 * j + p) * 48:(2 * j + p + 1) * 48] = part


def kernel(tile_rows, tiles, phases_ref, pairs_hbm, w_hbm, cls_hbm, out_ref,
           pairs_ref, w_ref, cls_ref, phase, blocks, recv, inc_ref, wpx_ref, lpx_ref, band, low, k_ref, sel_ref, tile_ref,
           z_ref, y_ref, x_ref, edge, halo_one, halo_two, halo_tile, acc,
           load_sem, own_sem, all_send, all_recv, send_sem, recv_sem):
    me, core = lax.axis_index("ifg"), lax.axis_index("tile")
    count = lax.axis_size("ifg")
    own = phase.shape[0]
    per = own // 2
    cols = phase.shape[2]
    left, right = lax.rem(me + count - 1, count), lax.rem(me + 1, count)
    has_left, has_right = me > 0, me < count - 1
    if tiles == 2:
        dirs = [(1 - core, None, jnp.where(core == 0, tile_rows - R, 0), jnp.where(core == 0, tile_rows, -R))]
    else:
        dirs = [(lax.rem(core + tiles - 1, tiles), core > 0, 0, -R),
                (lax.rem(core + 1, tiles), core < tiles - 1, tile_rows - R, tile_rows)]

    pieces = 2
    loads = []
    for i in range(pieces):
        for h in range(2):
            span = pl.ds(h * per + i * (per // pieces), per // pieces)
            loads.append(pltpu.make_async_copy(phases_ref.at[span], phase.at[span], load_sem.at[2 * i + h]))
            loads[-1].start()

    small = []
    for i, (src, dst) in enumerate(((pairs_hbm, pairs_ref), (w_hbm, w_ref), (cls_hbm, cls_ref))):
        small.append(pltpu.make_async_copy(src, dst, load_sem.at[4 + i]))
        small[-1].start()

    barrier = pltpu.get_barrier_semaphore()

    def greet(k, _):
        pl.semaphore_signal(barrier, inc=1, device_id=(lax.rem(me + k, count), core), device_id_type=MESH)
        return _

    lax.fori_loop(1, count, greet, 0)
    near = [[(me, tile), (left, tile), (right, tile)] for tile, _, _, _ in dirs]
    for group in near:
        for partner in group:
            pl.semaphore_signal(barrier, inc=1, device_id=partner, device_id_type=MESH)

    for i in range(pieces):
        loads[2 * i].wait()
        loads[2 * i + 1].wait()

        def turn(q, _):
            value = jnp.concatenate([phase[q], phase[q + per]], axis=0).T
            blocks[pl.ds(q, cols, stride=per), :] = value
            return _

        lax.fori_loop(i * (per // pieces), (i + 1) * (per // pieces), turn, 0, unroll=4)
    pl.semaphore_wait(barrier, count - 1 + 3 * len(dirs))

    spans = [(per, 2 * per), (0, per), (3 * per, per)]

    def exchange(i, k, src):
        peer = lax.rem(me + k, count)
        at, size = spans[i]
        return pltpu.make_async_remote_copy(
            src_ref=blocks.at[pl.ds(pl.multiple_of(peer * 4 * per + at, 8), size)], dst_ref=recv.at[src, pl.ds(at, size)],
            send_sem=all_send.at[i, k], recv_sem=all_recv.at[i, k], device_id=(peer, core), device_id_type=MESH)

    def send_first(k, _):
        exchange(0, k, me).start()
        return _

    def send_second(k, _, across):
        crosses = (lax.rem(me + k, count) >= count // 2) != (me >= count // 2)

        @pl.when(crosses if across else jnp.logical_not(crosses))
        def _start():
            exchange(1, k, me).start()
            exchange(2, k, me).start()

        return _

    lax.fori_loop(1, count, send_first, 0)
    mine = pltpu.make_async_copy(blocks.at[pl.ds(pl.multiple_of(me * 4 * per, 8), 4 * per)], recv.at[me], own_sem)
    mine.start()

    def absent(cond, *refs):
        @pl.when(jnp.logical_not(cond))
        def _():
            for ref in refs:
                ref[...] = jnp.zeros(ref.shape, F32)

    absent(has_left, halo_one.at[0], halo_two.at[0])
    absent(has_right, halo_one.at[1], halo_two.at[1])
    for p in range(2):
        for d, (_, has, _, _) in enumerate(dirs):
            absent(has_left if has is None else has_left & has, halo_tile.at[p, d, 0])
            absent(has_right if has is None else has_right & has, halo_tile.at[p, d, 2])
            if has is not None:
                absent(has, halo_tile.at[p, d, 1])

    for c in small:
        c.wait()
    prepare(pairs_ref, w_ref, cls_ref, per, count, inc_ref, wpx_ref, lpx_ref, band, low)
    fill_filters(dirs, one(has_left), one(has_right), k_ref, sel_ref, tile_ref)
    lax.fori_loop(1, count, functools.partial(send_second, across=False), 0)
    mine.wait()

    def take(group):
        def take_blocks(k, _):
            for i in group:
                exchange(i, k, lax.rem(me + count - k, count)).wait_recv()
            return _

        lax.fori_loop(1, count, take_blocks, 0)

    low_lanes = iota((ROWS, LANES), 1) < LANES // 2

    def right_side(p):
        values = []
        for c in PARTS[p]:
            got = recv[:, c * per:(c + 1) * per, :].reshape(count * per, LANES)
            values.append(got * wpx_ref[c])
        value = jnp.concatenate(split2(jnp.concatenate(values, axis=1)), axis=0)
        a, b = [dot_nn(inc_ref[h], value) for h in range(2)]
        for i in range(2):
            at = slice(i * LANES, (i + 1) * LANES)
            aa, ab, ba, bb = a[:ROWS, at], a[ROWS:, at], b[:ROWS, at], b[ROWS:, at]
            z_ref[pl.ds(i, ROWS, stride=2), :] = jnp.where(low_lanes, aa, bb) + swap(jnp.where(low_lanes, ab, ba))

    def forward(p):
        def step(t, a):
            at = pl.ds(t, 2)
            y = a[0]
            y_ref[at, :] = y * lpx_ref[p, 0, at, :]
            return [v - lpx_ref[p, j + 1, at, :] * y for j, v in enumerate(a[1:])]

        def block(b, carry):
            a = list(carry)
            base = pl.multiple_of(b * 16, 16)
            for s in range(8):
                a = step(base + 2 * s, a + [z_ref[pl.ds(base + 2 * s + 16, 2), :]])
            return tuple(a)

        a = list(lax.fori_loop(0, BLOCKS, block, tuple(z_ref[2 * t:2 * t + 2, :] for t in range(8))))
        for t in range(8 * BLOCKS, MEET):
            a = step(2 * t, a + [z_ref[2 * t + 16:2 * t + 18, :]])
        a = [a[j] + swap(a[7 - j]) for j in range(8)]
        for t in range(MEET, LAST):
            a = step(2 * t, a)

    def backward(p, send):
        one_ref, two_ref = x_ref.at[PARTS[p][0]], x_ref.at[PARTS[p][1]]

        def step(t, later, keep=True):
            at = pl.ds(2 * t, 2)
            value = y_ref[at, :]
            for g in range(len(later), 0, -1):
                value = value - lpx_ref[p, g, at, :] * later[g - 1]
            if keep:
                one_ref[pl.ds(t, 1), :] = value[0:1]
                two_ref[pl.ds(t, 1), :] = value[1:2]
            return [value] + later[:7]

        later = []
        for t in range(LAST - 1, 8 * BLOCKS - 1, -1):
            later = step(t, later, t < OUT)

        def block(b, carry):
            later = list(carry)
            base = pl.multiple_of(b * 8, 8)
            for s in range(7, -1, -1):
                later = step(base + s, later)
            return tuple(later)

        cut = CUT // 8
        carry = lax.fori_loop(0, BLOCKS - cut, lambda n, c: block(BLOCKS - 1 - n, c), tuple(later))
        send(0, pl.ds(CUT, OUT - CUT))
        lax.fori_loop(0, cut, lambda n, c: block(cut - 1 - n, c), carry)
        send(1, pl.ds(0, CUT))

    def copy(i, src, dst, device):
        return pltpu.make_async_remote_copy(src_ref=src, dst_ref=dst, send_sem=send_sem.at[i],
                                            recv_sem=recv_sem.at[i], device_id=device, device_id_type=MESH)

    sides = [[], []]

    def send_one(piece, span):
        src = x_ref.at[pl.ds(1, 2), span]
        sides[0].append(copy(2 * piece, src, halo_one.at[1, :, span], (left, core)))
        sides[1].append(copy(2 * piece + 1, src, halo_one.at[0, :, span], (right, core)))
        pl.when(has_left)(sides[0][-1].start)
        pl.when(has_right)(sides[1][-1].start)

    def send_two(piece, span):
        sides[0].append(copy(4 + 2 * piece, x_ref.at[0, span], halo_two.at[1, span], (left, core)))
        sides[1].append(copy(5 + 2 * piece, x_ref.at[3, span], halo_two.at[0, span], (right, core)))
        pl.when(has_left)(sides[0][-1].start)
        pl.when(has_right)(sides[1][-1].start)

    edges = []

    def both(a, b):
        return b if a is None else a if b is None else a & b

    def when(cond, action):
        action() if cond is None else pl.when(cond)(action)

    def solved(p):
        value = jnp.concatenate([x_ref[c] for c in PARTS[p]], axis=1)
        return split3(value)

    def send_edges(p, parts):
        for d, (_, has, _, _) in enumerate(dirs):
            edge[p, d] = dot_nt(sel_ref[d], jnp.concatenate(parts, axis=1))
            opposite = len(dirs) - 1 - d
            got = dirs[opposite][1]
            for i, (slot, to, came) in enumerate(((1, None, None), (2, has_left, has_right), (0, has_right, has_left))):
                c = copy(8 + (p * len(dirs) + d) * 3 + i, edge.at[p, d], halo_tile.at[p, opposite, slot], near[d][i])
                edges.append((c, both(has, to), both(got, came)))
                when(edges[-1][1], c.start)

    def apply(i, *values):
        wide = [v for high, middle, *_ in values for v in (high, middle, high)]
        return dot_nt(k_ref[:, 3 * WIDE * i:3 * WIDE * (i + len(values))], jnp.concatenate(wide, axis=1))

    def apply_tile():
        total = None
        for d in range(len(dirs)):
            pair = [split2(halo_tile[p, d].reshape(48, OUT)) for p in range(2)]
            order = [pair[0][0], pair[1][0], pair[0][1], pair[1][1], pair[0][0], pair[1][0]]
            term = dot_nn(tile_ref[d], jnp.concatenate(order, axis=0))
            total = term if total is None else total + term
        return total

    def wait_sides(first):
        for i in (2 * first, 2 * first + 1):
            pl.when(has_right)(sides[0][i].wait_recv)
            pl.when(has_left)(sides[1][i].wait_recv)

    take((0,))
    lax.fori_loop(1, count, functools.partial(send_second, across=True), 0)
    right_side(0)
    forward(0)
    backward(0, send_one)
    parts = solved(0)
    send_edges(0, parts)
    acc[...] = apply(0, parts)

    take((1, 2))
    right_side(1)
    forward(1)
    backward(1, send_two)
    parts = solved(1)
    send_edges(1, parts)
    wait_sides(0)
    for c, _, came in edges[:3 * len(dirs)]:
        when(came, c.wait_recv)
    beside = [split2(jnp.concatenate([halo_one[side, 0], halo_one[side, 1]], axis=1)) for side in range(2)]
    total = acc[...] + apply(1, parts, *beside)
    for c, _, came in edges[3 * len(dirs):]:
        when(came, c.wait_recv)
    total += apply_tile()
    wait_sides(1)
    total += apply(4, split2(jnp.concatenate([halo_two[0], halo_two[1]], axis=1)))

    front, back = total[:256], split2(total[256:])
    row, lane = iota((OUT, DATES), 0), iota((OUT, DATES), 1)
    turned = one((row < HALF) & (row == DATES - 1 - lane)).astype(BF16)
    later = dot_nn(back[0], turned) + dot_nn(back[1], turned)
    tail = jnp.where(iota((256, OUT - LANES), 1) < HALF - LANES, front[:, LANES:OUT], 0.0)
    first, second = front[:, 0:LANES], later[:, LANES:OUT] + tail
    for r in range(tile_rows):
        at = slice(4 * r, 4 * r + 4)
        out_ref[r, :, 0:LANES] = first[at]
        out_ref[r, :, LANES:DATES] = later[at, LANES:]
        out_ref[r, :, LANES:OUT] = second[at]

    def drain(k, _):
        for i in range(3):
            exchange(i, k, me).wait_send()
        return _

    lax.fori_loop(1, count, drain, 0)
    for has, group in ((has_left, sides[0]), (has_right, sides[1])):
        for c in group:
            pl.when(has)(c.wait_send)
    for c, went, _ in edges:
        when(went, c.wait_send)


def on_device(tiles, phases, pairs, class_weights, classes):
    own, tile_rows, cols = phases.shape
    tile_cols = classes.shape[1]
    count = cols // tile_cols
    assert tile_rows == 64 and tile_cols == 4
    if own % 16:
        more = -own % 16
        phases = jnp.pad(phases, ((0, more), (0, 0), (0, 0)))
        pairs = jnp.pad(pairs.reshape(count, own, 2), ((0, 0), (0, more), (0, 0))).reshape(-1, 2)
        class_weights = jnp.pad(class_weights.reshape(CLASSES, count, own), ((0, 0), (0, 0), (0, more))).reshape(CLASSES, -1)
        own += more
    nifg = pairs.shape[0]
    per = own // 2
    dirs = 1 if tiles == 2 else 2
    vmem = pl.BlockSpec(memory_space=pltpu.VMEM)
    copies = 8 + 6 * dirs

    corrected = pl.pallas_call(
        functools.partial(kernel, tile_rows, tiles),
        out_shape=jax.ShapeDtypeStruct((tile_rows, tile_cols, DATES), F32),
        in_specs=[pl.BlockSpec(memory_space=pltpu.HBM)] * 4,
        out_specs=vmem,
        scratch_shapes=[
            pltpu.VMEM((2, nifg), jnp.int32),
            pltpu.VMEM((CLASSES, nifg), F32),
            pltpu.VMEM((tile_cols, tile_rows), jnp.int32),
            pltpu.VMEM((own, tile_rows, cols), F32),
            pltpu.VMEM((cols * per, LANES), F32),
            pltpu.VMEM((count, 4 * per, LANES), F32),
            pltpu.VMEM((2, 2 * ROWS, nifg), BF16),
            pltpu.VMEM((4, nifg // 2, LANES), F32),
            pltpu.VMEM((2, MAXGAP + 1, 2 * ROWS, LANES), F32),
            pltpu.VMEM((MAXGAP + 1, ROWS, LANES), F32),
            pltpu.VMEM((MAXGAP + 1, ROWS, LANES), F32),
            pltpu.VMEM((2 * 256, 15 * WIDE), BF16),
            pltpu.VMEM((dirs, 16, 3 * WIDE), BF16),
            pltpu.VMEM((dirs, 2 * 256, 6 * 48), BF16),
            pltpu.VMEM((2 * ROWS, LANES), F32),
            pltpu.VMEM((2 * ROWS, LANES), F32),
            pltpu.VMEM((4, OUT, LANES), F32),
            pltpu.VMEM((2, dirs, 16, OUT), F32),
            pltpu.VMEM((2, 2, OUT, LANES), F32),
            pltpu.VMEM((2, OUT, LANES), F32),
            pltpu.VMEM((2, dirs, 3, 16, OUT), F32),
            pltpu.VMEM((2 * 256, OUT), F32),
            pltpu.SemaphoreType.DMA((7,)),
            pltpu.SemaphoreType.DMA,
            pltpu.SemaphoreType.DMA((3, count)),
            pltpu.SemaphoreType.DMA((3, count)),
            pltpu.SemaphoreType.DMA((copies,)),
            pltpu.SemaphoreType.DMA((copies,)),
        ],
        compiler_params=pltpu.CompilerParams(
            collective_id=0, has_side_effects=True, vmem_limit_bytes=58 * 1024 * 1024
        ),
        name="invert_and_filter",
    )(phases, pairs.T, class_weights, classes.T)
    return corrected


def solution(mesh):
    return jax.shard_map(
        functools.partial(on_device, mesh.shape["tile"]),
        mesh=mesh,
        in_specs=(P("ifg", "tile", None), P(), P(), P("tile", "ifg")),
        out_specs=P("tile", "ifg", None),
        check_vma=False,
    )
```

```python
import functools
import math
import jax
import jax.numpy as jnp
from jax import lax
from jax.experimental import pallas as pl
from jax.experimental.pallas import tpu as pltpu
from jax.sharding import PartitionSpec as P

DATES = 300
CLASSES = 8
MAXGAP = 8
R = 3
LANES = 128
WIDE = 2 * LANES
HALF = DATES // 2
MEET = HALF - MAXGAP // 2
LAST = MEET + MAXGAP
ROWS = -(-LAST // 16) * 16
OUT = -(-HALF // 8) * 8
CUT = (OUT // 16) * 8
BLOCKS = MEET // 8
PARTS = ((1, 2), (0, 3))
GROUPS = ((1,), (2,), (0, 3))
MESH = pl.DeviceIdType.MESH

smooth_weight = 1.0
anchor_weight = 0.1

NORM = sum(math.exp(-j * j / 4.5) for j in range(-R, R + 1))
F32, BF16 = jnp.float32, jnp.bfloat16


def split3(value):
    high = value.astype(BF16)
    rest = value - high.astype(F32)
    middle = rest.astype(BF16)
    low = (rest - middle.astype(F32)).astype(BF16)
    return (high, middle, low)


def split2(value):
    high = value.astype(BF16)
    return high, (value - high.astype(F32)).astype(BF16)


def dot_nt(a, b):
    return lax.dot_general(a, b, (((1,), (1,)), ((), ())), preferred_element_type=F32)


def dot_nn(a, b):
    return lax.dot_general(a, b, (((1,), (0,)), ((), ())), preferred_element_type=F32)


def iota(shape, dim):
    return lax.broadcasted_iota(jnp.int32, shape, dim)


def one(cond):
    return jnp.where(cond, 1.0, 0.0)


def tap(delta):
    near = jnp.exp((delta * delta).astype(F32) * (-1.0 / 4.5)) * (1.0 / NORM)
    return jnp.where(jnp.abs(delta) <= R, near, 0.0)


def tap_at(delta):
    return math.exp(-delta * delta / 4.5) / NORM if abs(delta) <= R else 0.0


def spread(start, size, stride):
    return pl.ds(start, size, stride=stride) if stride > 1 else pl.ds(start, size)


def swap(value):
    return pltpu.roll(value, LANES // 2, 1)


def bands(pairs_ref, w_ref, band):
    nifg = pairs_ref.shape[1]
    first, second = pairs_ref[0:1, :], pairs_ref[1:2, :]
    gap = second - first
    row = iota((ROWS, nifg), 0)
    left = [one(row == first), one(row == second), one(DATES - 1 - row == second), one(DATES - 1 - row == first)]
    left = jnp.concatenate(left, axis=0).astype(BF16)
    w = w_ref[...]
    zero = jnp.zeros((CLASSES, nifg), F32)
    grouped = [jnp.where(gap == g, w, 0.0) for g in range(1, MAXGAP + 1)] + [w] + [zero] * 7
    high, middle, low = split3(jnp.concatenate(grouped, axis=0))
    both = dot_nt(left, jnp.concatenate([high, middle], axis=0))
    total = both[:, :LANES] + (both[:, LANES:] + dot_nt(left, low))
    ff, fs, bs, bf = [total[i * ROWS:(i + 1) * ROWS] for i in range(4)]
    lane = iota((ROWS, LANES), 1)
    t = iota((ROWS, LANES), 0)
    front, used = lane < LANES // 2, (lane & (LANES // 2 - 1)) < CLASSES
    band[0] = jnp.where(used, jnp.where(front, swap(ff + fs), bs + bf), 0.0) + (
        smooth_weight * (1.0 + 4.0 * one(t >= 1) + one(t >= 2)) + anchor_weight)
    off = jnp.where(front, ff, swap(bs))
    for g in range(1, MAXGAP + 1):
        here = off if g == 1 else pltpu.roll(off, LANES - 8 * (g - 1), 1)
        here = -jnp.where(used, here, 0.0)
        if g == 1:
            here += smooth_weight * (-2.0 - 2.0 * one(t >= 1))
        elif g == 2:
            here += smooth_weight
        band[g] = jnp.where(t + g < LAST, here, 0.0)


def factor(band, low):
    zero = jnp.zeros((1, LANES), F32)
    keys = [(j, h) for j in range(MAXGAP) for h in range(MAXGAP - j)]

    def step(at, acc):
        c = [band[h, at, :] for h in range(MAXGAP + 1)]
        c = [c[h] - acc[(0, h)] for h in range(MAXGAP)] + [c[MAXGAP]]
        inv = 1.0 / c[0]
        low[0, at, :] = inv
        fresh = {}
        for j in range(1, MAXGAP + 1):
            lj = c[j] * inv
            low[j, at, :] = lj
            for h in range(MAXGAP - j + 1):
                term = lj * c[j + h]
                old = acc.get((j, h))
                fresh[(j - 1, h)] = term if old is None else old + term
        return fresh

    def block(b, carry):
        acc = dict(zip(keys, carry))
        base = pl.multiple_of(b * 8, 8)
        for s in range(8):
            acc = step(pl.ds(base + s, 1), acc)
        return tuple(acc[k] for k in keys)

    acc = dict(zip(keys, lax.fori_loop(0, BLOCKS, block, tuple(zero for _ in keys))))
    for t in range(8 * BLOCKS, MEET):
        acc = step(pl.ds(t, 1), acc)
    acc = {(j, h): acc[(j, h)] + swap(acc[(MAXGAP - 1 - j - h, h)]) for j, h in keys}
    for t in range(MEET, LAST):
        acc = step(pl.ds(t, 1), acc)


def prepare(pairs_ref, w_ref, cls_ref, await_theirs, theirs_ref, per, count, inc_ref, wpx_ref, lpx_ref, band, low):
    nifg = pairs_ref.shape[1]
    half = nifg // 2
    q, lane = iota((LANES, LANES), 0), iota((LANES, LANES), 1)
    local = q & 63
    place = (local < 3 * CLASSES) & ((q >= 64) == (lane >= 64))

    def members(ref, columns):
        classes = ref[...]
        classes = jnp.concatenate([classes, classes], axis=1)
        each = [one(place & ((local & 7) == classes[c:c + 1, :])) for c in columns]
        return jnp.concatenate(each, axis=1).astype(BF16)

    onehot = members(cls_ref, range(4))

    parts = [p.astype(F32) for p in split3(w_ref[...])]
    ends = [jnp.broadcast_to(pairs_ref[i:i + 1, :].astype(F32), (8, nifg)) for i in range(2)]
    stack = jnp.concatenate(parts + ends + [jnp.zeros((24, nifg), F32)], axis=0)
    by_ifg = jnp.concatenate([stack, stack], axis=0).T.reshape(count, 2 * per, LANES)
    ours, others = by_ifg[:, :per].reshape(half, LANES), by_ifg[:, per:].reshape(half, LANES)
    packed = jnp.where(iota((half, LANES), 1) < 64, ours, others)
    await_theirs()
    every = jnp.concatenate([onehot, members(theirs_ref, PARTS[1])], axis=1)
    weights = dot_nn(packed.astype(BF16), every)
    for c in range(6):
        wpx_ref[c] = weights[:, c * LANES:(c + 1) * LANES]
    ends = packed.T
    row = iota((ROWS, half), 0)
    inside = row < HALF
    row = row.astype(F32)
    for h in range(2):
        first, second = ends[64 * h + 24:64 * h + 25, :], ends[64 * h + 32:64 * h + 33, :]
        front = one(inside & (row == second)) - one(inside & (row == first))
        back = one(inside & (DATES - 1.0 - row == second)) - one(inside & (DATES - 1.0 - row == first))
        both = jnp.concatenate([front, back], axis=0).astype(BF16)
        inc_ref[h, :, 0:half] = both
        inc_ref[h, :, half:] = both

    bands(pairs_ref, w_ref, band)
    factor(band, low)
    used = (iota((ROWS, LANES), 1) & 63) < CLASSES
    valid = iota((ROWS, LANES), 0) < LAST
    for g in range(MAXGAP + 1):
        high, middle, rest = [p.astype(F32) for p in split3(jnp.where(used & valid, low[g], 0.0))]
        value = high + pltpu.roll(middle, 8, 1) + pltpu.roll(rest, 16, 1)
        each = dot_nn(value.astype(BF16), onehot)
        for p, columns in enumerate(GROUPS):
            for i, c in enumerate(columns):
                lpx_ref[p, g, spread(i, ROWS, len(columns)), :] = each[:, c * LANES:(c + 1) * LANES]


def fill_filters(dirs, has_left, has_right, k_ref, sel_ref, tile_ref):
    shape = (2 * 256, LANES)
    row, lane = iota(shape, 0), iota(shape, 1)
    out_c, out_r = row & 3, (row & 255) >> 2
    match = (row >= 256) == (lane >= 64)
    delta = out_r - (lane & 63)
    vertical = jnp.where(match, tap(delta), 0.0)
    straight = one(match & (delta == 0))

    def column(at, has):
        taps = [tap_at(c - at) for c in range(4)]
        near = jnp.where(out_c == 0, taps[0], jnp.where(out_c == 1, taps[1], jnp.where(out_c == 2, taps[2], taps[3])))
        value = -vertical * near
        if 0 <= at < 4:
            value += jnp.where(out_c == at, straight, 0.0)
        return value if has is None else value * has

    sets = [(1, None, 2, None), (0, None, 3, None), (-3, has_left, -2, has_left), (5, has_right, 6, has_right), (-1, has_left, 4, has_right)]
    for i, (a, has_a, b, has_b) in enumerate(sets):
        high, middle = split2(jnp.concatenate([column(a, has_a), column(b, has_b)], axis=1))
        for j, part in enumerate((high, high, middle)):
            k_ref[:, (3 * i + j) * WIDE:(3 * i + j + 1) * WIDE] = part
    for d, (_, _, sent, _) in enumerate(dirs):
        shape = (16, 3 * WIDE)
        row, lane = iota(shape, 0), iota(shape, 1) & (WIDE - 1)
        pick = ((row >> 2) == (lane >> 6)) & ((row & 3) < R) & ((lane & 63) == sent + (row & 3))
        sel_ref[d] = one(pick).astype(BF16)
    for p, columns in enumerate(PARTS):
        for d, (_, has, _, got) in enumerate(dirs):
            shape = (2 * 256, 48)
            row, lane = iota(shape, 0), iota(shape, 1)
            side, slot = lane >> 4, lane & 15
            col = jnp.where((slot >> 3) == 0, columns[0], columns[1]) + 4 * (side - 1)
            out_c, out_r = row & 3, (row & 255) >> 2
            ok = ((slot & 3) < R) & (((slot >> 2) & 1) == (row >> 8))
            value = jnp.where(ok, -tap(out_r - got - (slot & 3)) * tap(out_c - col), 0.0)
            there = jnp.where(side == 0, has_left, jnp.where(side == 2, has_right, 1.0))
            value = value * there if has is None else value * there * one(has)
            high, middle = split2(value)
            for j, part in enumerate((high, high, middle)):
                tile_ref[d, :, (2 * j + p) * 48:(2 * j + p + 1) * 48] = part


def kernel(tile_rows, tiles, phases_ref, pairs_hbm, w_hbm, cls_hbm, out_ref,
           pairs_ref, w_ref, cls_ref, phase, blocks, recv, inc_ref, wpx_ref, lpx_ref, band, low, k_ref, sel_ref, tile_ref,
           z_ref, z_sent, z_got, theirs_ref, y_ref, x_ref, edge, halo_one, halo_two, halo_tile, acc,
           load_sem, own_sem, first_send, first_recv, near_send, near_recv, pair_send, pair_recv, send_sem, recv_sem):
    me, core = lax.axis_index("ifg"), lax.axis_index("tile")
    count = lax.axis_size("ifg")
    own = phase.shape[0]
    per = own // 2
    cols = phase.shape[2]
    left, right = lax.rem(me + count - 1, count), lax.rem(me + 1, count)
    has_left, has_right = me > 0, me < count - 1
    if tiles == 2:
        dirs = [(1 - core, None, jnp.where(core == 0, tile_rows - R, 0), jnp.where(core == 0, tile_rows, -R))]
    else:
        dirs = [(lax.rem(core + tiles - 1, tiles), core > 0, 0, -R),
                (lax.rem(core + 1, tiles), core < tiles - 1, tile_rows - R, tile_rows)]

    pieces = 2
    loads = []
    for i in range(pieces):
        for h in range(2):
            span = pl.ds(h * per + i * (per // pieces), per // pieces)
            loads.append(pltpu.make_async_copy(phases_ref.at[span], phase.at[span], load_sem.at[2 * i + h]))
            loads[-1].start()

    small = []
    for i, (src, dst) in enumerate(((pairs_hbm, pairs_ref), (w_hbm, w_ref), (cls_hbm, cls_ref))):
        small.append(pltpu.make_async_copy(src, dst, load_sem.at[4 + i]))
        small[-1].start()

    barrier = pltpu.get_barrier_semaphore()

    def greet(k, _):
        pl.semaphore_signal(barrier, inc=1, device_id=(lax.rem(me + k, count), core), device_id_type=MESH)
        return _

    lax.fori_loop(1, count, greet, 0)
    near = [[(me, tile), (left, tile), (right, tile)] for tile, _, _, _ in dirs]
    for group in near:
        for partner in group:
            pl.semaphore_signal(barrier, inc=1, device_id=partner, device_id_type=MESH)

    for i in range(pieces):
        loads[2 * i].wait()
        loads[2 * i + 1].wait()

        def turn(q, _):
            value = jnp.concatenate([phase[q], phase[q + per]], axis=0).T
            blocks[pl.ds(q, cols, stride=per), :] = value
            return _

        lax.fori_loop(i * (per // pieces), (i + 1) * (per // pieces), turn, 0, unroll=4)
    pl.semaphore_wait(barrier, count - 1 + 3 * len(dirs))

    half = count // 2
    base = jnp.where(me >= half, half, 0)
    away = half - base
    place = me - base
    partner = away + place

    def remote(src, dst, send, recv_at, device):
        return pltpu.make_async_remote_copy(src_ref=src, dst_ref=dst, send_sem=send, recv_sem=recv_at,
                                            device_id=(device, core), device_id_type=MESH)

    def block_of(owner, at, size):
        return blocks.at[pl.ds(pl.multiple_of(owner * 4 * per + at, 8), size)]

    def first_copy(j, far, src, c):
        start, i = (away, j) if far else (base, half + j)
        peer = start + lax.rem(place + j, half)
        return remote(block_of(peer, c * per, per), recv.at[src, pl.ds(c * per, per)], first_send.at[c - 1, i], first_recv.at[c - 1, i], peer)

    def near_copy(i, j, src):
        peer = lax.rem(place + j, half)
        at = 3 * per * (i % 2)
        owner, slot = (base + peer, base + src) if i < 2 else (away + peer, away + src)
        return remote(block_of(owner, at, per), recv.at[slot, pl.ds(at, per)], near_send.at[i, j], near_recv.at[i, j], base + peer)

    def each(begin, action):
        def body(j, _):
            action(j)
            return _

        lax.fori_loop(begin, half, body, 0)

    def source(j):
        return lax.rem(place + half - j, half)

    def near_start(kinds):
        def action(j):
            for i in kinds:
                near_copy(i, j, place).start()

        each(1, action)

    def near_wait(kinds):
        def action(j):
            for i in kinds:
                near_copy(i, j, source(j)).wait_recv()

        each(1, action)

    theirs = remote(cls_ref, theirs_ref, pair_send.at[2], pair_recv.at[2], partner)
    small[2].wait()
    theirs.start()
    each(0, lambda j: first_copy(j, True, me, 1).start())
    each(1, lambda j: first_copy(j, False, me, 1).start())
    near_start((2, 3))
    each(0, lambda j: first_copy(j, True, me, 2).start())
    each(1, lambda j: first_copy(j, False, me, 2).start())
    mine = [pltpu.make_async_copy(block_of(me, 0, 4 * per), recv.at[me], own_sem.at[0])]
    for i in range(2):
        at = 3 * per * i
        mine.append(pltpu.make_async_copy(block_of(partner, at, per), recv.at[partner, pl.ds(at, per)], own_sem.at[1 + i]))
    for c in mine:
        c.start()

    def absent(cond, *refs):
        @pl.when(jnp.logical_not(cond))
        def _():
            for ref in refs:
                ref[...] = jnp.zeros(ref.shape, F32)

    absent(has_left, halo_one.at[0], halo_two.at[0])
    absent(has_right, halo_one.at[1], halo_two.at[1])
    for p in range(2):
        for d, (_, has, _, _) in enumerate(dirs):
            absent(has_left if has is None else has_left & has, halo_tile.at[p, d, 0])
            absent(has_right if has is None else has_right & has, halo_tile.at[p, d, 2])
            if has is not None:
                absent(has, halo_tile.at[p, d, 1])

    for c in small[:2]:
        c.wait()
    prepare(pairs_ref, w_ref, cls_ref, theirs.wait_recv, theirs_ref, per, count, inc_ref, wpx_ref, lpx_ref, band, low)
    fill_filters(dirs, one(has_left), one(has_right), k_ref, sel_ref, tile_ref)
    for c in mine:
        c.wait()

    def take_first(c):
        each(0, lambda j: first_copy(j, True, away + source(j), c).wait_recv())
        each(1, lambda j: first_copy(j, False, base + source(j), c).wait_recv())

    low_lanes = iota((ROWS, LANES), 1) < LANES // 2

    def sums(values, left_sides):
        value = jnp.concatenate(split2(jnp.concatenate(values, axis=1)), axis=0)
        a, b = [dot_nn(side, value) for side in left_sides]
        packed = []
        for i in range(len(values)):
            at = slice(i * LANES, (i + 1) * LANES)
            aa, ab, ba, bb = a[:ROWS, at], a[ROWS:, at], b[:ROWS, at], b[ROWS:, at]
            packed.append(jnp.where(low_lanes, aa, bb) + swap(jnp.where(low_lanes, ab, ba)))
        return packed

    def first_side(c):
        value = recv[:, c * per:(c + 1) * per, :].reshape(count * per, LANES) * wpx_ref[c]
        z_ref[0:ROWS, :] = sums([value], [inc_ref[h] for h in range(2)])[0]

    def half_side(slots, weights):
        size = half * per
        span = pl.ds(pl.multiple_of(base * per, LANES), size)
        values = []
        for c, w in zip(PARTS[1], weights):
            got = recv[pl.ds(slots, half), c * per:(c + 1) * per, :].reshape(size, LANES)
            values.append(got * wpx_ref[w, span, :])
        sides = [inc_ref[h, :, span] for h in range(2)]
        return sums(values, [jnp.concatenate([side, side], axis=1) for side in sides])

    def forward(p):
        n = len(GROUPS[p])

        def step(t, a):
            at = pl.ds(t, n)
            y = a[0]
            y_ref[at, :] = y * lpx_ref[p, 0, at, :]
            return [v - lpx_ref[p, j + 1, at, :] * y for j, v in enumerate(a[1:])]

        def block(b, carry):
            a = list(carry)
            base = pl.multiple_of(b * 8 * n, 8 * n)
            for s in range(8):
                a = step(base + n * s, a + [z_ref[pl.ds(base + n * (s + 8), n), :]])
            return tuple(a)

        a = list(lax.fori_loop(0, BLOCKS, block, tuple(z_ref[n * t:n * t + n, :] for t in range(8))))
        for t in range(8 * BLOCKS, MEET):
            a = step(n * t, a + [z_ref[n * (t + 8):n * (t + 9), :]])
        a = [a[j] + swap(a[7 - j]) for j in range(8)]
        for t in range(MEET, LAST):
            a = step(n * t, a)

    def backward(p, send):
        n = len(GROUPS[p])
        refs = [x_ref.at[c] for c in GROUPS[p]]

        def step(t, later, keep=True):
            at = pl.ds(n * t, n)
            value = y_ref[at, :]
            for g in range(len(later), 0, -1):
                value = value - lpx_ref[p, g, at, :] * later[g - 1]
            if keep:
                for i, ref in enumerate(refs):
                    ref[pl.ds(t, 1), :] = value[i:i + 1]
            return [value] + later[:7]

        later = []
        for t in range(LAST - 1, 8 * BLOCKS - 1, -1):
            later = step(t, later, t < OUT)

        def block(b, carry):
            later = list(carry)
            base = pl.multiple_of(b * 8, 8)
            for s in range(7, -1, -1):
                later = step(base + s, later)
            return tuple(later)

        cut = CUT // 8
        carry = lax.fori_loop(0, BLOCKS - cut, lambda n, c: block(BLOCKS - 1 - n, c), tuple(later))
        send(0, pl.ds(CUT, OUT - CUT))
        lax.fori_loop(0, cut, lambda n, c: block(cut - 1 - n, c), carry)
        send(1, pl.ds(0, CUT))

    def copy(i, src, dst, device):
        return pltpu.make_async_remote_copy(src_ref=src, dst_ref=dst, send_sem=send_sem.at[i],
                                            recv_sem=recv_sem.at[i], device_id=device, device_id_type=MESH)

    sides = [[], []]

    def send_one(c):
        def send(piece, span):
            at = 4 * (c - 1) + 2 * piece
            src = x_ref.at[c, span]
            sides[0].append(copy(at, src, halo_one.at[1, c - 1, span], (left, core)))
            sides[1].append(copy(at + 1, src, halo_one.at[0, c - 1, span], (right, core)))
            pl.when(has_left)(sides[0][-1].start)
            pl.when(has_right)(sides[1][-1].start)

        return send

    def send_two(piece, span):
        sides[0].append(copy(8 + 2 * piece, x_ref.at[0, span], halo_two.at[1, span], (left, core)))
        sides[1].append(copy(9 + 2 * piece, x_ref.at[3, span], halo_two.at[0, span], (right, core)))
        pl.when(has_left)(sides[0][-1].start)
        pl.when(has_right)(sides[1][-1].start)

    edges = []

    def both(a, b):
        return b if a is None else a if b is None else a & b

    def when(cond, action):
        action() if cond is None else pl.when(cond)(action)

    def solved(p):
        value = jnp.concatenate([x_ref[c] for c in PARTS[p]], axis=1)
        return split3(value)

    def send_edges(p, parts):
        for d, (_, has, _, _) in enumerate(dirs):
            edge[p, d] = dot_nt(sel_ref[d], jnp.concatenate(parts, axis=1))
            opposite = len(dirs) - 1 - d
            got = dirs[opposite][1]
            for i, (slot, to, came) in enumerate(((1, None, None), (2, has_left, has_right), (0, has_right, has_left))):
                c = copy(12 + (p * len(dirs) + d) * 3 + i, edge.at[p, d], halo_tile.at[p, opposite, slot], near[d][i])
                edges.append((c, both(has, to), both(got, came)))
                when(edges[-1][1], c.start)

    def apply(i, *values):
        wide = [v for high, middle, *_ in values for v in (high, middle, high)]
        return dot_nt(k_ref[:, 3 * WIDE * i:3 * WIDE * (i + len(values))], jnp.concatenate(wide, axis=1))

    def apply_tile():
        total = None
        for d in range(len(dirs)):
            pair = [split2(halo_tile[p, d].reshape(48, OUT)) for p in range(2)]
            order = [pair[0][0], pair[1][0], pair[0][1], pair[1][1], pair[0][0], pair[1][0]]
            term = dot_nn(tile_ref[d], jnp.concatenate(order, axis=0))
            total = term if total is None else total + term
        return total

    def wait_sides(begin, end):
        for i in range(begin, end):
            pl.when(has_right)(sides[0][i].wait_recv)
            pl.when(has_left)(sides[1][i].wait_recv)

    take_first(1)
    first_side(1)
    forward(0)
    backward(0, send_one(1))
    near_start((0, 1))
    near_wait((2, 3))
    for i, z in enumerate(half_side(away, (4, 5))):
        z_sent[i] = z[:OUT]
    summed = [remote(z_sent.at[i], z_got.at[i], pair_send.at[i], pair_recv.at[i], partner) for i in range(2)]
    take_first(2)
    for c in summed:
        c.start()
    first_side(2)
    forward(1)
    backward(1, send_one(2))
    parts = solved(0)
    send_edges(0, parts)
    acc[...] = apply(0, parts)

    near_wait((0, 1))
    nearby = half_side(base, PARTS[1])
    for i, z in enumerate(nearby):
        summed[i].wait_recv()
        z_ref[pl.ds(i, OUT, stride=2), :] = z[:OUT] + z_got[i]
        z_ref[pl.ds(2 * OUT + i, ROWS - OUT, stride=2), :] = z[OUT:]
    forward(2)
    backward(2, send_two)
    parts = solved(1)
    send_edges(1, parts)
    wait_sides(0, 4)
    for c, _, came in edges[:3 * len(dirs)]:
        when(came, c.wait_recv)
    beside = [split2(jnp.concatenate([halo_one[side, 0], halo_one[side, 1]], axis=1)) for side in range(2)]
    total = acc[...] + apply(1, parts, *beside)
    for c, _, came in edges[3 * len(dirs):]:
        when(came, c.wait_recv)
    total += apply_tile()
    wait_sides(4, 6)
    total += apply(4, split2(jnp.concatenate([halo_two[0], halo_two[1]], axis=1)))

    front, back = total[:256], split2(total[256:])
    row, lane = iota((OUT, DATES), 0), iota((OUT, DATES), 1)
    turned = one((row < HALF) & (row == DATES - 1 - lane)).astype(BF16)
    later = dot_nn(back[0], turned) + dot_nn(back[1], turned)
    tail = jnp.where(iota((256, OUT - LANES), 1) < HALF - LANES, front[:, LANES:OUT], 0.0)
    first, second = front[:, 0:LANES], later[:, LANES:OUT] + tail
    for r in range(tile_rows):
        at = slice(4 * r, 4 * r + 4)
        out_ref[r, :, 0:LANES] = first[at]
        out_ref[r, :, LANES:DATES] = later[at, LANES:]
        out_ref[r, :, LANES:OUT] = second[at]

    def sent(j, far):
        for c in PARTS[0]:
            first_copy(j, far, me, c).wait_send()
        if not far:
            for i in range(4):
                near_copy(i, j, place).wait_send()

    each(0, functools.partial(sent, far=True))
    each(1, functools.partial(sent, far=False))
    for c in [theirs] + summed:
        c.wait_send()
    for has, group in ((has_left, sides[0]), (has_right, sides[1])):
        for c in group:
            pl.when(has)(c.wait_send)
    for c, went, _ in edges:
        when(went, c.wait_send)


def on_device(tiles, phases, pairs, class_weights, classes):
    own, tile_rows, cols = phases.shape
    tile_cols = classes.shape[1]
    count = cols // tile_cols
    assert tile_rows == 64 and tile_cols == 4 and count % 2 == 0
    if own % 16:
        more = -own % 16
        phases = jnp.pad(phases, ((0, more), (0, 0), (0, 0)))
        pairs = jnp.pad(pairs.reshape(count, own, 2), ((0, 0), (0, more), (0, 0))).reshape(-1, 2)
        class_weights = jnp.pad(class_weights.reshape(CLASSES, count, own), ((0, 0), (0, 0), (0, more))).reshape(CLASSES, -1)
        own += more
    nifg = pairs.shape[0]
    per = own // 2
    dirs = 1 if tiles == 2 else 2
    vmem = pl.BlockSpec(memory_space=pltpu.VMEM)
    copies = 12 + 6 * dirs

    corrected = pl.pallas_call(
        functools.partial(kernel, tile_rows, tiles),
        out_shape=jax.ShapeDtypeStruct((tile_rows, tile_cols, DATES), F32),
        in_specs=[pl.BlockSpec(memory_space=pltpu.HBM)] * 4,
        out_specs=vmem,
        scratch_shapes=[
            pltpu.VMEM((2, nifg), jnp.int32),
            pltpu.VMEM((CLASSES, nifg), F32),
            pltpu.VMEM((tile_cols, tile_rows), jnp.int32),
            pltpu.VMEM((own, tile_rows, cols), F32),
            pltpu.VMEM((cols * per, LANES), F32),
            pltpu.VMEM((count, 4 * per, LANES), F32),
            pltpu.VMEM((2, 2 * ROWS, nifg), BF16),
            pltpu.VMEM((6, nifg // 2, LANES), F32),
            pltpu.VMEM((3, MAXGAP + 1, 2 * ROWS, LANES), F32),
            pltpu.VMEM((MAXGAP + 1, ROWS, LANES), F32),
            pltpu.VMEM((MAXGAP + 1, ROWS, LANES), F32),
            pltpu.VMEM((2 * 256, 15 * WIDE), BF16),
            pltpu.VMEM((dirs, 16, 3 * WIDE), BF16),
            pltpu.VMEM((dirs, 2 * 256, 6 * 48), BF16),
            pltpu.VMEM((2 * ROWS, LANES), F32),
            pltpu.VMEM((2, OUT, LANES), F32),
            pltpu.VMEM((2, OUT, LANES), F32),
            pltpu.VMEM((tile_cols, tile_rows), jnp.int32),
            pltpu.VMEM((2 * ROWS, LANES), F32),
            pltpu.VMEM((4, OUT, LANES), F32),
            pltpu.VMEM((2, dirs, 16, OUT), F32),
            pltpu.VMEM((2, 2, OUT, LANES), F32),
            pltpu.VMEM((2, OUT, LANES), F32),
            pltpu.VMEM((2, dirs, 3, 16, OUT), F32),
            pltpu.VMEM((2 * 256, OUT), F32),
            pltpu.SemaphoreType.DMA((7,)),
            pltpu.SemaphoreType.DMA((3,)),
            pltpu.SemaphoreType.DMA((2, count)),
            pltpu.SemaphoreType.DMA((2, count)),
            pltpu.SemaphoreType.DMA((4, count // 2)),
            pltpu.SemaphoreType.DMA((4, count // 2)),
            pltpu.SemaphoreType.DMA((3,)),
            pltpu.SemaphoreType.DMA((3,)),
            pltpu.SemaphoreType.DMA((copies,)),
            pltpu.SemaphoreType.DMA((copies,)),
        ],
        compiler_params=pltpu.CompilerParams(
            collective_id=0, has_side_effects=True, vmem_limit_bytes=58 * 1024 * 1024
        ),
        name="invert_and_filter",
    )(phases, pairs.T, class_weights, classes.T)
    return corrected


def solution(mesh):
    return jax.shard_map(
        functools.partial(on_device, mesh.shape["tile"]),
        mesh=mesh,
        in_specs=(P("ifg", "tile", None), P(), P(), P("tile", "ifg")),
        out_specs=P("tile", "ifg", None),
        check_vma=False,
    )
```

```python
import functools
import math
import jax
import jax.numpy as jnp
from jax import lax
from jax.experimental import pallas as pl
from jax.experimental.pallas import tpu as pltpu
from jax.sharding import PartitionSpec as P

DATES = 300
CLASSES = 8
MAXGAP = 8
R = 3
LANES = 128
WIDE = 2 * LANES
HALF = DATES // 2
MEET = HALF - MAXGAP // 2
LAST = MEET + MAXGAP
ROWS = -(-LAST // 16) * 16
OUT = -(-HALF // 8) * 8
CUT = (OUT // 16) * 8
BLOCKS = MEET // 8
PARTS = ((1, 2), (0, 3))
GROUPS = ((1,), (2,), (0, 3))
MESH = pl.DeviceIdType.MESH

smooth_weight = 1.0
anchor_weight = 0.1

NORM = sum(math.exp(-j * j / 4.5) for j in range(-R, R + 1))
F32, BF16 = jnp.float32, jnp.bfloat16


def split3(value):
    high = value.astype(BF16)
    rest = value - high.astype(F32)
    middle = rest.astype(BF16)
    low = (rest - middle.astype(F32)).astype(BF16)
    return (high, middle, low)


def split2(value):
    high = value.astype(BF16)
    return high, (value - high.astype(F32)).astype(BF16)


def dot_nt(a, b):
    return lax.dot_general(a, b, (((1,), (1,)), ((), ())), preferred_element_type=F32)


def dot_nn(a, b):
    return lax.dot_general(a, b, (((1,), (0,)), ((), ())), preferred_element_type=F32)


def iota(shape, dim):
    return lax.broadcasted_iota(jnp.int32, shape, dim)


def one(cond):
    return jnp.where(cond, 1.0, 0.0)


def tap(delta):
    near = jnp.exp((delta * delta).astype(F32) * (-1.0 / 4.5)) * (1.0 / NORM)
    return jnp.where(jnp.abs(delta) <= R, near, 0.0)


def tap_at(delta):
    return math.exp(-delta * delta / 4.5) / NORM if abs(delta) <= R else 0.0


def spread(start, size, stride):
    return pl.ds(start, size, stride=stride) if stride > 1 else pl.ds(start, size)


def swap(value):
    return pltpu.roll(value, LANES // 2, 1)


def bands(pairs_ref, w_ref, band):
    nifg = pairs_ref.shape[1]
    first, second = pairs_ref[0:1, :], pairs_ref[1:2, :]
    gap = second - first
    row = iota((ROWS, nifg), 0)
    left = [one(row == first), one(row == second), one(DATES - 1 - row == second), one(DATES - 1 - row == first)]
    left = jnp.concatenate(left, axis=0).astype(BF16)
    w = w_ref[...]
    zero = jnp.zeros((CLASSES, nifg), F32)
    grouped = [jnp.where(gap == g, w, 0.0) for g in range(1, MAXGAP + 1)] + [w] + [zero] * 7
    high, middle, low = split3(jnp.concatenate(grouped, axis=0))
    both = dot_nt(left, jnp.concatenate([high, middle], axis=0))
    total = both[:, :LANES] + (both[:, LANES:] + dot_nt(left, low))
    ff, fs, bs, bf = [total[i * ROWS:(i + 1) * ROWS] for i in range(4)]
    lane = iota((ROWS, LANES), 1)
    t = iota((ROWS, LANES), 0)
    front, used = lane < LANES // 2, (lane & (LANES // 2 - 1)) < CLASSES
    band[0] = jnp.where(used, jnp.where(front, swap(ff + fs), bs + bf), 0.0) + (
        smooth_weight * (1.0 + 4.0 * one(t >= 1) + one(t >= 2)) + anchor_weight)
    off = jnp.where(front, ff, swap(bs))
    for g in range(1, MAXGAP + 1):
        here = off if g == 1 else pltpu.roll(off, LANES - 8 * (g - 1), 1)
        here = -jnp.where(used, here, 0.0)
        if g == 1:
            here += smooth_weight * (-2.0 - 2.0 * one(t >= 1))
        elif g == 2:
            here += smooth_weight
        band[g] = jnp.where(t + g < LAST, here, 0.0)


def factor(band, low):
    zero = jnp.zeros((1, LANES), F32)
    keys = [(j, h) for j in range(MAXGAP) for h in range(MAXGAP - j)]

    def step(at, acc):
        c = [band[h, at, :] for h in range(MAXGAP + 1)]
        c = [c[h] - acc[(0, h)] for h in range(MAXGAP)] + [c[MAXGAP]]
        inv = 1.0 / c[0]
        low[0, at, :] = inv
        fresh = {}
        for j in range(1, MAXGAP + 1):
            lj = c[j] * inv
            low[j, at, :] = lj
            for h in range(MAXGAP - j + 1):
                term = lj * c[j + h]
                old = acc.get((j, h))
                fresh[(j - 1, h)] = term if old is None else old + term
        return fresh

    def block(b, carry):
        acc = dict(zip(keys, carry))
        base = pl.multiple_of(b * 8, 8)
        for s in range(8):
            acc = step(pl.ds(base + s, 1), acc)
        return tuple(acc[k] for k in keys)

    acc = dict(zip(keys, lax.fori_loop(0, BLOCKS, block, tuple(zero for _ in keys))))
    for t in range(8 * BLOCKS, MEET):
        acc = step(pl.ds(t, 1), acc)
    acc = {(j, h): acc[(j, h)] + swap(acc[(MAXGAP - 1 - j - h, h)]) for j, h in keys}
    for t in range(MEET, LAST):
        acc = step(pl.ds(t, 1), acc)


def prepare(pairs_ref, w_ref, cls_ref, await_theirs, theirs_ref, per, count, inc_ref, wpx_ref, lpx_ref, band, low):
    nifg = pairs_ref.shape[1]
    half = nifg // 2
    q, lane = iota((LANES, LANES), 0), iota((LANES, LANES), 1)
    local = q & 63
    place = (local < 3 * CLASSES) & ((q >= 64) == (lane >= 64))

    def members(ref, columns):
        classes = ref[...]
        classes = jnp.concatenate([classes, classes], axis=1)
        each = [one(place & ((local & 7) == classes[c:c + 1, :])) for c in columns]
        return jnp.concatenate(each, axis=1).astype(BF16)

    onehot = members(cls_ref, range(4))

    parts = [p.astype(F32) for p in split3(w_ref[...])]
    ends = [jnp.broadcast_to(pairs_ref[i:i + 1, :].astype(F32), (8, nifg)) for i in range(2)]
    stack = jnp.concatenate(parts + ends + [jnp.zeros((24, nifg), F32)], axis=0)
    by_ifg = jnp.concatenate([stack, stack], axis=0).T.reshape(count, 2 * per, LANES)
    ours, others = by_ifg[:, :per].reshape(half, LANES), by_ifg[:, per:].reshape(half, LANES)
    packed = jnp.where(iota((half, LANES), 1) < 64, ours, others)
    await_theirs()
    every = jnp.concatenate([onehot, members(theirs_ref, PARTS[1])], axis=1)
    weights = dot_nn(packed.astype(BF16), every)
    for c in range(6):
        wpx_ref[c] = weights[:, c * LANES:(c + 1) * LANES]
    ends = packed.T
    row = iota((ROWS, half), 0)
    inside = row < HALF
    row = row.astype(F32)
    for h in range(2):
        first, second = ends[64 * h + 24:64 * h + 25, :], ends[64 * h + 32:64 * h + 33, :]
        front = one(inside & (row == second)) - one(inside & (row == first))
        back = one(inside & (DATES - 1.0 - row == second)) - one(inside & (DATES - 1.0 - row == first))
        both = jnp.concatenate([front, back], axis=0).astype(BF16)
        inc_ref[h, :, 0:half] = both
        inc_ref[h, :, half:] = both

    bands(pairs_ref, w_ref, band)
    factor(band, low)
    used = (iota((ROWS, LANES), 1) & 63) < CLASSES
    valid = iota((ROWS, LANES), 0) < LAST
    for g in range(MAXGAP + 1):
        high, middle, rest = [p.astype(F32) for p in split3(jnp.where(used & valid, low[g], 0.0))]
        value = high + pltpu.roll(middle, 8, 1) + pltpu.roll(rest, 16, 1)
        each = dot_nn(value.astype(BF16), onehot)
        for p, columns in enumerate(GROUPS):
            for i, c in enumerate(columns):
                lpx_ref[p, g, spread(i, ROWS, len(columns)), :] = each[:, c * LANES:(c + 1) * LANES]


def fill_filters(dirs, has_left, has_right, k_ref, sel_ref, tile_ref):
    shape = (2 * 256, LANES)
    row, lane = iota(shape, 0), iota(shape, 1)
    out_c, out_r = row & 3, (row & 255) >> 2
    match = (row >= 256) == (lane >= 64)
    delta = out_r - (lane & 63)
    vertical = jnp.where(match, tap(delta), 0.0)
    straight = one(match & (delta == 0))

    def column(at, has):
        taps = [tap_at(c - at) for c in range(4)]
        near = jnp.where(out_c == 0, taps[0], jnp.where(out_c == 1, taps[1], jnp.where(out_c == 2, taps[2], taps[3])))
        value = -vertical * near
        if 0 <= at < 4:
            value += jnp.where(out_c == at, straight, 0.0)
        return value if has is None else value * has

    sets = [(1, None, 2, None), (0, None, 3, None), (-3, has_left, -2, has_left), (5, has_right, 6, has_right), (-1, has_left, 4, has_right)]
    for i, (a, has_a, b, has_b) in enumerate(sets):
        high, middle = split2(jnp.concatenate([column(a, has_a), column(b, has_b)], axis=1))
        for j, part in enumerate((high, high, middle)):
            k_ref[:, (3 * i + j) * WIDE:(3 * i + j + 1) * WIDE] = part
    for d, (_, _, sent, _) in enumerate(dirs):
        shape = (16, 3 * WIDE)
        row, lane = iota(shape, 0), iota(shape, 1) & (WIDE - 1)
        pick = ((row >> 2) == (lane >> 6)) & ((row & 3) < R) & ((lane & 63) == sent + (row & 3))
        sel_ref[d] = one(pick).astype(BF16)
    for p, columns in enumerate(PARTS):
        for d, (_, has, _, got) in enumerate(dirs):
            shape = (2 * 256, 48)
            row, lane = iota(shape, 0), iota(shape, 1)
            side, slot = lane >> 4, lane & 15
            col = jnp.where((slot >> 3) == 0, columns[0], columns[1]) + 4 * (side - 1)
            out_c, out_r = row & 3, (row & 255) >> 2
            ok = ((slot & 3) < R) & (((slot >> 2) & 1) == (row >> 8))
            value = jnp.where(ok, -tap(out_r - got - (slot & 3)) * tap(out_c - col), 0.0)
            there = jnp.where(side == 0, has_left, jnp.where(side == 2, has_right, 1.0))
            value = value * there if has is None else value * there * one(has)
            high, middle = split2(value)
            for j, part in enumerate((high, high, middle)):
                tile_ref[d, :, (2 * j + p) * 48:(2 * j + p + 1) * 48] = part


def kernel(tile_rows, tiles, phases_ref, pairs_hbm, w_hbm, cls_hbm, out_ref,
           pairs_ref, w_ref, cls_ref, phase, blocks, recv, inc_ref, wpx_ref, lpx_ref, band, low, k_ref, sel_ref, tile_ref,
           z_ref, z_sent, z_got, theirs_ref, y_ref, x_ref, edge, halo_one, halo_two, halo_tile, acc,
           load_sem, own_sem, first_send, first_recv, near_send, near_recv, pair_send, pair_recv, send_sem, recv_sem):
    me, core = lax.axis_index("ifg"), lax.axis_index("tile")
    count = lax.axis_size("ifg")
    own = phase.shape[0]
    per = own // 2
    cols = phase.shape[2]
    left, right = lax.rem(me + count - 1, count), lax.rem(me + 1, count)
    has_left, has_right = me > 0, me < count - 1
    if tiles == 2:
        dirs = [(1 - core, None, jnp.where(core == 0, tile_rows - R, 0), jnp.where(core == 0, tile_rows, -R))]
    else:
        dirs = [(lax.rem(core + tiles - 1, tiles), core > 0, 0, -R),
                (lax.rem(core + 1, tiles), core < tiles - 1, tile_rows - R, tile_rows)]

    pieces = 4
    loads = []
    for i in range(pieces):
        for h in range(2):
            span = pl.ds(h * per + i * (per // pieces), per // pieces)
            loads.append(pltpu.make_async_copy(phases_ref.at[span], phase.at[span], load_sem.at[2 * i + h]))
            loads[-1].start()

    small = []
    for i, (src, dst) in enumerate(((pairs_hbm, pairs_ref), (w_hbm, w_ref), (cls_hbm, cls_ref))):
        small.append(pltpu.make_async_copy(src, dst, load_sem.at[8 + i]))
        small[-1].start()

    barrier = pltpu.get_barrier_semaphore()

    def greet(k, _):
        pl.semaphore_signal(barrier, inc=1, device_id=(lax.rem(me + k, count), core), device_id_type=MESH)
        return _

    lax.fori_loop(1, count, greet, 0)
    near = [[(me, tile), (left, tile), (right, tile)] for tile, _, _, _ in dirs]
    for group in near:
        for partner in group:
            pl.semaphore_signal(barrier, inc=1, device_id=partner, device_id_type=MESH)

    for i in range(pieces):
        loads[2 * i].wait()
        loads[2 * i + 1].wait()

        def turn(q, _):
            value = jnp.concatenate([phase[q], phase[q + per]], axis=0).T
            blocks[pl.ds(q, cols, stride=per), :] = value
            return _

        lax.fori_loop(i * (per // pieces), (i + 1) * (per // pieces), turn, 0, unroll=4)
    pl.semaphore_wait(barrier, count - 1 + 3 * len(dirs))

    half = count // 2
    base = jnp.where(me >= half, half, 0)
    away = half - base
    place = me - base
    partner = away + place

    def remote(src, dst, send, recv_at, device):
        return pltpu.make_async_remote_copy(src_ref=src, dst_ref=dst, send_sem=send, recv_sem=recv_at,
                                            device_id=(device, core), device_id_type=MESH)

    def block_of(owner, at, size):
        return blocks.at[pl.ds(pl.multiple_of(owner * 4 * per + at, 8), size)]

    def first_copy(j, far, src, c):
        start, i = (away, j) if far else (base, half + j)
        peer = start + lax.rem(place + j, half)
        return remote(block_of(peer, c * per, per), recv.at[src, pl.ds(c * per, per)], first_send.at[c - 1, i], first_recv.at[c - 1, i], peer)

    def near_copy(i, j, src):
        peer = lax.rem(place + j, half)
        at = 3 * per * (i % 2)
        owner, slot = (base + peer, base + src) if i < 2 else (away + peer, away + src)
        return remote(block_of(owner, at, per), recv.at[slot, pl.ds(at, per)], near_send.at[i, j], near_recv.at[i, j], base + peer)

    def each(begin, action):
        def body(j, _):
            action(j)
            return _

        lax.fori_loop(begin, half, body, 0)

    def source(j):
        return lax.rem(place + half - j, half)

    def near_start(kinds):
        def action(j):
            for i in kinds:
                near_copy(i, j, place).start()

        each(1, action)

    def near_wait(kinds):
        def action(j):
            for i in kinds:
                near_copy(i, j, source(j)).wait_recv()

        each(1, action)

    theirs = remote(cls_ref, theirs_ref, pair_send.at[2], pair_recv.at[2], partner)
    small[2].wait()
    theirs.start()
    each(0, lambda j: first_copy(j, True, me, 1).start())
    each(1, lambda j: first_copy(j, False, me, 1).start())
    near_start((2, 3))
    each(0, lambda j: first_copy(j, True, me, 2).start())
    each(1, lambda j: first_copy(j, False, me, 2).start())
    mine = [pltpu.make_async_copy(block_of(me, 0, 4 * per), recv.at[me], own_sem.at[0])]
    for i in range(2):
        at = 3 * per * i
        mine.append(pltpu.make_async_copy(block_of(partner, at, per), recv.at[partner, pl.ds(at, per)], own_sem.at[1 + i]))
    for c in mine:
        c.start()

    def absent(cond, *refs):
        @pl.when(jnp.logical_not(cond))
        def _():
            for ref in refs:
                ref[...] = jnp.zeros(ref.shape, F32)

    absent(has_left, halo_one.at[0], halo_two.at[0])
    absent(has_right, halo_one.at[1], halo_two.at[1])
    for p in range(2):
        for d, (_, has, _, _) in enumerate(dirs):
            absent(has_left if has is None else has_left & has, halo_tile.at[p, d, 0])
            absent(has_right if has is None else has_right & has, halo_tile.at[p, d, 2])
            if has is not None:
                absent(has, halo_tile.at[p, d, 1])

    for c in small[:2]:
        c.wait()
    prepare(pairs_ref, w_ref, cls_ref, theirs.wait_recv, theirs_ref, per, count, inc_ref, wpx_ref, lpx_ref, band, low)
    fill_filters(dirs, one(has_left), one(has_right), k_ref, sel_ref, tile_ref)
    for c in mine:
        c.wait()

    def take_first(c):
        each(0, lambda j: first_copy(j, True, away + source(j), c).wait_recv())
        each(1, lambda j: first_copy(j, False, base + source(j), c).wait_recv())

    low_lanes = iota((ROWS, LANES), 1) < LANES // 2

    def sums(values, left_sides):
        value = jnp.concatenate(split2(jnp.concatenate(values, axis=1)), axis=0)
        a, b = [dot_nn(side, value) for side in left_sides]
        packed = []
        for i in range(len(values)):
            at = slice(i * LANES, (i + 1) * LANES)
            aa, ab, ba, bb = a[:ROWS, at], a[ROWS:, at], b[:ROWS, at], b[ROWS:, at]
            packed.append(jnp.where(low_lanes, aa, bb) + swap(jnp.where(low_lanes, ab, ba)))
        return packed

    def first_side(c):
        value = recv[:, c * per:(c + 1) * per, :].reshape(count * per, LANES) * wpx_ref[c]
        z_ref[0:ROWS, :] = sums([value], [inc_ref[h] for h in range(2)])[0]

    def half_side(slots, weights):
        size = half * per
        span = pl.ds(pl.multiple_of(base * per, LANES), size)
        values = []
        for c, w in zip(PARTS[1], weights):
            got = recv[pl.ds(slots, half), c * per:(c + 1) * per, :].reshape(size, LANES)
            values.append(got * wpx_ref[w, span, :])
        sides = [inc_ref[h, :, span] for h in range(2)]
        return sums(values, [jnp.concatenate([side, side], axis=1) for side in sides])

    def forward(p):
        n = len(GROUPS[p])

        def step(t, a):
            at = pl.ds(t, n)
            y = a[0]
            y_ref[at, :] = y * lpx_ref[p, 0, at, :]
            return [v - lpx_ref[p, j + 1, at, :] * y for j, v in enumerate(a[1:])]

        def block(b, carry):
            a = list(carry)
            base = pl.multiple_of(b * 8 * n, 8 * n)
            for s in range(8):
                a = step(base + n * s, a + [z_ref[pl.ds(base + n * (s + 8), n), :]])
            return tuple(a)

        a = list(lax.fori_loop(0, BLOCKS, block, tuple(z_ref[n * t:n * t + n, :] for t in range(8))))
        for t in range(8 * BLOCKS, MEET):
            a = step(n * t, a + [z_ref[n * (t + 8):n * (t + 9), :]])
        a = [a[j] + swap(a[7 - j]) for j in range(8)]
        for t in range(MEET, LAST):
            a = step(n * t, a)

    def backward(p, send):
        n = len(GROUPS[p])
        refs = [x_ref.at[c] for c in GROUPS[p]]

        def step(t, later, keep=True):
            at = pl.ds(n * t, n)
            value = y_ref[at, :]
            for g in range(len(later), 0, -1):
                value = value - lpx_ref[p, g, at, :] * later[g - 1]
            if keep:
                for i, ref in enumerate(refs):
                    ref[pl.ds(t, 1), :] = value[i:i + 1]
            return [value] + later[:7]

        later = []
        for t in range(LAST - 1, 8 * BLOCKS - 1, -1):
            later = step(t, later, t < OUT)

        def block(b, carry):
            later = list(carry)
            base = pl.multiple_of(b * 8, 8)
            for s in range(7, -1, -1):
                later = step(base + s, later)
            return tuple(later)

        cut = CUT // 8
        carry = lax.fori_loop(0, BLOCKS - cut, lambda n, c: block(BLOCKS - 1 - n, c), tuple(later))
        send(0, pl.ds(CUT, OUT - CUT))
        lax.fori_loop(0, cut, lambda n, c: block(cut - 1 - n, c), carry)
        send(1, pl.ds(0, CUT))

    def copy(i, src, dst, device):
        return pltpu.make_async_remote_copy(src_ref=src, dst_ref=dst, send_sem=send_sem.at[i],
                                            recv_sem=recv_sem.at[i], device_id=device, device_id_type=MESH)

    sides = [[], []]

    def send_one(c):
        def send(piece, span):
            at = 4 * (c - 1) + 2 * piece
            src = x_ref.at[c, span]
            sides[0].append(copy(at, src, halo_one.at[1, c - 1, span], (left, core)))
            sides[1].append(copy(at + 1, src, halo_one.at[0, c - 1, span], (right, core)))
            pl.when(has_left)(sides[0][-1].start)
            pl.when(has_right)(sides[1][-1].start)

        return send

    def send_two(piece, span):
        sides[0].append(copy(8 + 2 * piece, x_ref.at[0, span], halo_two.at[1, span], (left, core)))
        sides[1].append(copy(9 + 2 * piece, x_ref.at[3, span], halo_two.at[0, span], (right, core)))
        pl.when(has_left)(sides[0][-1].start)
        pl.when(has_right)(sides[1][-1].start)

    edges = []

    def both(a, b):
        return b if a is None else a if b is None else a & b

    def when(cond, action):
        action() if cond is None else pl.when(cond)(action)

    def solved(p):
        value = jnp.concatenate([x_ref[c] for c in PARTS[p]], axis=1)
        return split3(value)

    def send_edges(p, parts):
        for d, (_, has, _, _) in enumerate(dirs):
            edge[p, d] = dot_nt(sel_ref[d], jnp.concatenate(parts, axis=1))
            opposite = len(dirs) - 1 - d
            got = dirs[opposite][1]
            for i, (slot, to, came) in enumerate(((1, None, None), (2, has_left, has_right), (0, has_right, has_left))):
                c = copy(12 + (p * len(dirs) + d) * 3 + i, edge.at[p, d], halo_tile.at[p, opposite, slot], near[d][i])
                edges.append((c, both(has, to), both(got, came)))
                when(edges[-1][1], c.start)

    def apply(i, *values):
        wide = [v for high, middle, *_ in values for v in (high, middle, high)]
        return dot_nt(k_ref[:, 3 * WIDE * i:3 * WIDE * (i + len(values))], jnp.concatenate(wide, axis=1))

    def apply_tile():
        total = None
        for d in range(len(dirs)):
            pair = [split2(halo_tile[p, d].reshape(48, OUT)) for p in range(2)]
            order = [pair[0][0], pair[1][0], pair[0][1], pair[1][1], pair[0][0], pair[1][0]]
            term = dot_nn(tile_ref[d], jnp.concatenate(order, axis=0))
            total = term if total is None else total + term
        return total

    def wait_sides(begin, end):
        for i in range(begin, end):
            pl.when(has_right)(sides[0][i].wait_recv)
            pl.when(has_left)(sides[1][i].wait_recv)

    take_first(1)
    first_side(1)
    forward(0)
    backward(0, send_one(1))
    near_wait((2, 3))
    for i, z in enumerate(half_side(away, (4, 5))):
        z_sent[i] = z[:OUT]
    summed = [remote(z_sent.at[i], z_got.at[i], pair_send.at[i], pair_recv.at[i], partner) for i in range(2)]
    for c in summed:
        c.start()
    near_start((0, 1))
    take_first(2)
    first_side(2)
    forward(1)
    backward(1, send_one(2))
    parts = solved(0)
    send_edges(0, parts)
    acc[...] = apply(0, parts)

    near_wait((0, 1))
    nearby = half_side(base, PARTS[1])
    for i, z in enumerate(nearby):
        summed[i].wait_recv()
        z_ref[pl.ds(i, OUT, stride=2), :] = z[:OUT] + z_got[i]
        z_ref[pl.ds(2 * OUT + i, ROWS - OUT, stride=2), :] = z[OUT:]
    forward(2)
    backward(2, send_two)
    parts = solved(1)
    send_edges(1, parts)
    wait_sides(0, 4)
    for c, _, came in edges[:3 * len(dirs)]:
        when(came, c.wait_recv)
    beside = [split2(jnp.concatenate([halo_one[side, 0], halo_one[side, 1]], axis=1)) for side in range(2)]
    total = acc[...] + apply(1, parts, *beside)
    for c, _, came in edges[3 * len(dirs):]:
        when(came, c.wait_recv)
    total += apply_tile()
    wait_sides(4, 6)
    total += apply(4, split2(jnp.concatenate([halo_two[0], halo_two[1]], axis=1)))

    front, back = total[:256], split2(total[256:])
    row, lane = iota((OUT, DATES), 0), iota((OUT, DATES), 1)
    turned = one((row < HALF) & (row == DATES - 1 - lane)).astype(BF16)
    later = dot_nn(back[0], turned) + dot_nn(back[1], turned)
    tail = jnp.where(iota((256, OUT - LANES), 1) < HALF - LANES, front[:, LANES:OUT], 0.0)
    first, second = front[:, 0:LANES], later[:, LANES:OUT] + tail
    for r in range(tile_rows):
        at = slice(4 * r, 4 * r + 4)
        out_ref[r, :, 0:LANES] = first[at]
        out_ref[r, :, LANES:DATES] = later[at, LANES:]
        out_ref[r, :, LANES:OUT] = second[at]

    def sent(j, far):
        for c in PARTS[0]:
            first_copy(j, far, me, c).wait_send()
        if not far:
            for i in range(4):
                near_copy(i, j, place).wait_send()

    each(0, functools.partial(sent, far=True))
    each(1, functools.partial(sent, far=False))
    for c in [theirs] + summed:
        c.wait_send()
    for has, group in ((has_left, sides[0]), (has_right, sides[1])):
        for c in group:
            pl.when(has)(c.wait_send)
    for c, went, _ in edges:
        when(went, c.wait_send)


def on_device(tiles, phases, pairs, class_weights, classes):
    own, tile_rows, cols = phases.shape
    tile_cols = classes.shape[1]
    count = cols // tile_cols
    assert tile_rows == 64 and tile_cols == 4 and count % 2 == 0
    if own % 16:
        more = -own % 16
        phases = jnp.pad(phases, ((0, more), (0, 0), (0, 0)))
        pairs = jnp.pad(pairs.reshape(count, own, 2), ((0, 0), (0, more), (0, 0))).reshape(-1, 2)
        class_weights = jnp.pad(class_weights.reshape(CLASSES, count, own), ((0, 0), (0, 0), (0, more))).reshape(CLASSES, -1)
        own += more
    nifg = pairs.shape[0]
    per = own // 2
    dirs = 1 if tiles == 2 else 2
    vmem = pl.BlockSpec(memory_space=pltpu.VMEM)
    copies = 12 + 6 * dirs

    corrected = pl.pallas_call(
        functools.partial(kernel, tile_rows, tiles),
        out_shape=jax.ShapeDtypeStruct((tile_rows, tile_cols, DATES), F32),
        in_specs=[pl.BlockSpec(memory_space=pltpu.HBM)] * 4,
        out_specs=vmem,
        scratch_shapes=[
            pltpu.VMEM((2, nifg), jnp.int32),
            pltpu.VMEM((CLASSES, nifg), F32),
            pltpu.VMEM((tile_cols, tile_rows), jnp.int32),
            pltpu.VMEM((own, tile_rows, cols), F32),
            pltpu.VMEM((cols * per, LANES), F32),
            pltpu.VMEM((count, 4 * per, LANES), F32),
            pltpu.VMEM((2, 2 * ROWS, nifg), BF16),
            pltpu.VMEM((6, nifg // 2, LANES), F32),
            pltpu.VMEM((3, MAXGAP + 1, 2 * ROWS, LANES), F32),
            pltpu.VMEM((MAXGAP + 1, ROWS, LANES), F32),
            pltpu.VMEM((MAXGAP + 1, ROWS, LANES), F32),
            pltpu.VMEM((2 * 256, 15 * WIDE), BF16),
            pltpu.VMEM((dirs, 16, 3 * WIDE), BF16),
            pltpu.VMEM((dirs, 2 * 256, 6 * 48), BF16),
            pltpu.VMEM((2 * ROWS, LANES), F32),
            pltpu.VMEM((2, OUT, LANES), F32),
            pltpu.VMEM((2, OUT, LANES), F32),
            pltpu.VMEM((tile_cols, tile_rows), jnp.int32),
            pltpu.VMEM((2 * ROWS, LANES), F32),
            pltpu.VMEM((4, OUT, LANES), F32),
            pltpu.VMEM((2, dirs, 16, OUT), F32),
            pltpu.VMEM((2, 2, OUT, LANES), F32),
            pltpu.VMEM((2, OUT, LANES), F32),
            pltpu.VMEM((2, dirs, 3, 16, OUT), F32),
            pltpu.VMEM((2 * 256, OUT), F32),
            pltpu.SemaphoreType.DMA((11,)),
            pltpu.SemaphoreType.DMA((3,)),
            pltpu.SemaphoreType.DMA((2, count)),
            pltpu.SemaphoreType.DMA((2, count)),
            pltpu.SemaphoreType.DMA((4, count // 2)),
            pltpu.SemaphoreType.DMA((4, count // 2)),
            pltpu.SemaphoreType.DMA((3,)),
            pltpu.SemaphoreType.DMA((3,)),
            pltpu.SemaphoreType.DMA((copies,)),
            pltpu.SemaphoreType.DMA((copies,)),
        ],
        compiler_params=pltpu.CompilerParams(
            collective_id=0, has_side_effects=True, vmem_limit_bytes=58 * 1024 * 1024
        ),
        name="invert_and_filter",
    )(phases, pairs.T, class_weights, classes.T)
    return corrected


def solution(mesh):
    return jax.shard_map(
        functools.partial(on_device, mesh.shape["tile"]),
        mesh=mesh,
        in_specs=(P("ifg", "tile", None), P(), P(), P("tile", "ifg")),
        out_specs=P("tile", "ifg", None),
        check_vma=False,
    )
```

```python
import functools
import math
import jax
import jax.numpy as jnp
from jax import lax
from jax.experimental import pallas as pl
from jax.experimental.pallas import tpu as pltpu
from jax.sharding import PartitionSpec as P

DATES = 300
CLASSES = 8
MAXGAP = 8
R = 3
LANES = 128
WIDE = 2 * LANES
HALF = DATES // 2
MEET = HALF - MAXGAP // 2
LAST = MEET + MAXGAP
ROWS = -(-LAST // 16) * 16
OUT = -(-HALF // 8) * 8
CUT = (OUT // 16) * 8
BLOCKS = MEET // 8
PARTS = ((1, 2), (0, 3))
GROUPS = ((1,), (2,), (0, 3))
MESH = pl.DeviceIdType.MESH

smooth_weight = 1.0
anchor_weight = 0.1

NORM = sum(math.exp(-j * j / 4.5) for j in range(-R, R + 1))
F32, BF16 = jnp.float32, jnp.bfloat16


def split3(value):
    high = value.astype(BF16)
    rest = value - high.astype(F32)
    middle = rest.astype(BF16)
    low = (rest - middle.astype(F32)).astype(BF16)
    return (high, middle, low)


def split2(value):
    high = value.astype(BF16)
    return high, (value - high.astype(F32)).astype(BF16)


def dot_nt(a, b):
    return lax.dot_general(a, b, (((1,), (1,)), ((), ())), preferred_element_type=F32)


def dot_nn(a, b):
    return lax.dot_general(a, b, (((1,), (0,)), ((), ())), preferred_element_type=F32)


def iota(shape, dim):
    return lax.broadcasted_iota(jnp.int32, shape, dim)


def one(cond):
    return jnp.where(cond, 1.0, 0.0)


def tap(delta):
    near = jnp.exp((delta * delta).astype(F32) * (-1.0 / 4.5)) * (1.0 / NORM)
    return jnp.where(jnp.abs(delta) <= R, near, 0.0)


def tap_at(delta):
    return math.exp(-delta * delta / 4.5) / NORM if abs(delta) <= R else 0.0


def spread(start, size, stride):
    return pl.ds(start, size, stride=stride) if stride > 1 else pl.ds(start, size)


def swap(value):
    return pltpu.roll(value, LANES // 2, 1)


def bands(pairs_ref, w_ref, band):
    nifg = pairs_ref.shape[1]
    first, second = pairs_ref[0:1, :], pairs_ref[1:2, :]
    gap = second - first
    row = iota((ROWS, nifg), 0)
    left = [one(row == first), one(row == second), one(DATES - 1 - row == second), one(DATES - 1 - row == first)]
    left = jnp.concatenate(left, axis=0).astype(BF16)
    w = w_ref[...]
    zero = jnp.zeros((CLASSES, nifg), F32)
    grouped = [jnp.where(gap == g, w, 0.0) for g in range(1, MAXGAP + 1)] + [w] + [zero] * 7
    high, middle, low = split3(jnp.concatenate(grouped, axis=0))
    both = dot_nt(left, jnp.concatenate([high, middle], axis=0))
    total = both[:, :LANES] + (both[:, LANES:] + dot_nt(left, low))
    ff, fs, bs, bf = [total[i * ROWS:(i + 1) * ROWS] for i in range(4)]
    lane = iota((ROWS, LANES), 1)
    t = iota((ROWS, LANES), 0)
    front, used = lane < LANES // 2, (lane & (LANES // 2 - 1)) < CLASSES
    band[0] = jnp.where(used, jnp.where(front, swap(ff + fs), bs + bf), 0.0) + (
        smooth_weight * (1.0 + 4.0 * one(t >= 1) + one(t >= 2)) + anchor_weight)
    off = jnp.where(front, ff, swap(bs))
    for g in range(1, MAXGAP + 1):
        here = off if g == 1 else pltpu.roll(off, LANES - 8 * (g - 1), 1)
        here = -jnp.where(used, here, 0.0)
        if g == 1:
            here += smooth_weight * (-2.0 - 2.0 * one(t >= 1))
        elif g == 2:
            here += smooth_weight
        band[g] = jnp.where(t + g < LAST, here, 0.0)


def factor(band, low):
    zero = jnp.zeros((1, LANES), F32)
    keys = [(j, h) for j in range(MAXGAP) for h in range(MAXGAP - j)]

    def step(at, acc):
        c = [band[h, at, :] for h in range(MAXGAP + 1)]
        c = [c[h] - acc[(0, h)] for h in range(MAXGAP)] + [c[MAXGAP]]
        inv = 1.0 / c[0]
        low[0, at, :] = inv
        fresh = {}
        for j in range(1, MAXGAP + 1):
            lj = c[j] * inv
            low[j, at, :] = lj
            for h in range(MAXGAP - j + 1):
                term = lj * c[j + h]
                old = acc.get((j, h))
                fresh[(j - 1, h)] = term if old is None else old + term
        return fresh

    def block(b, carry):
        acc = dict(zip(keys, carry))
        base = pl.multiple_of(b * 8, 8)
        for s in range(8):
            acc = step(pl.ds(base + s, 1), acc)
        return tuple(acc[k] for k in keys)

    acc = dict(zip(keys, lax.fori_loop(0, BLOCKS, block, tuple(zero for _ in keys))))
    for t in range(8 * BLOCKS, MEET):
        acc = step(pl.ds(t, 1), acc)
    acc = {(j, h): acc[(j, h)] + swap(acc[(MAXGAP - 1 - j - h, h)]) for j, h in keys}
    for t in range(MEET, LAST):
        acc = step(pl.ds(t, 1), acc)


def prepare(pairs_ref, w_ref, cls_ref, await_theirs, theirs_ref, per, count, inc_ref, wpx_ref, lpx_ref, band, low):
    nifg = pairs_ref.shape[1]
    half = nifg // 2
    q, lane = iota((LANES, LANES), 0), iota((LANES, LANES), 1)
    local = q & 63
    place = (local < 3 * CLASSES) & ((q >= 64) == (lane >= 64))

    def members(ref, columns):
        classes = ref[...]
        classes = jnp.concatenate([classes, classes], axis=1)
        each = [one(place & ((local & 7) == classes[c:c + 1, :])) for c in columns]
        return jnp.concatenate(each, axis=1).astype(BF16)

    onehot = members(cls_ref, range(4))

    parts = [p.astype(F32) for p in split3(w_ref[...])]
    ends = [jnp.broadcast_to(pairs_ref[i:i + 1, :].astype(F32), (8, nifg)) for i in range(2)]
    stack = jnp.concatenate(parts + ends + [jnp.zeros((24, nifg), F32)], axis=0)
    by_ifg = jnp.concatenate([stack, stack], axis=0).T.reshape(count, 2 * per, LANES)
    ours, others = by_ifg[:, :per].reshape(half, LANES), by_ifg[:, per:].reshape(half, LANES)
    packed = jnp.where(iota((half, LANES), 1) < 64, ours, others)
    await_theirs()
    every = jnp.concatenate([onehot, members(theirs_ref, PARTS[1])], axis=1)
    weights = dot_nn(packed.astype(BF16), every)
    for c in range(6):
        wpx_ref[c] = weights[:, c * LANES:(c + 1) * LANES]
    ends = packed.T
    row = iota((ROWS, half), 0)
    inside = row < HALF
    row = row.astype(F32)
    for h in range(2):
        first, second = ends[64 * h + 24:64 * h + 25, :], ends[64 * h + 32:64 * h + 33, :]
        front = one(inside & (row == second)) - one(inside & (row == first))
        back = one(inside & (DATES - 1.0 - row == second)) - one(inside & (DATES - 1.0 - row == first))
        both = jnp.concatenate([front, back], axis=0).astype(BF16)
        inc_ref[h, :, 0:half] = both
        inc_ref[h, :, half:] = both

    bands(pairs_ref, w_ref, band)
    factor(band, low)
    used = (iota((ROWS, LANES), 1) & 63) < CLASSES
    valid = iota((ROWS, LANES), 0) < LAST
    for g in range(MAXGAP + 1):
        high, middle, rest = [p.astype(F32) for p in split3(jnp.where(used & valid, low[g], 0.0))]
        value = high + pltpu.roll(middle, 8, 1) + pltpu.roll(rest, 16, 1)
        each = dot_nn(value.astype(BF16), onehot)
        for p, columns in enumerate(GROUPS):
            for i, c in enumerate(columns):
                lpx_ref[p, g, spread(i, ROWS, len(columns)), :] = each[:, c * LANES:(c + 1) * LANES]


def fill_filters(dirs, has_left, has_right, k_ref, sel_ref, tile_ref):
    shape = (2 * 256, LANES)
    row, lane = iota(shape, 0), iota(shape, 1)
    out_c, out_r = row & 3, (row & 255) >> 2
    match = (row >= 256) == (lane >= 64)
    delta = out_r - (lane & 63)
    vertical = jnp.where(match, tap(delta), 0.0)
    straight = one(match & (delta == 0))

    def column(at, has):
        taps = [tap_at(c - at) for c in range(4)]
        near = jnp.where(out_c == 0, taps[0], jnp.where(out_c == 1, taps[1], jnp.where(out_c == 2, taps[2], taps[3])))
        value = -vertical * near
        if 0 <= at < 4:
            value += jnp.where(out_c == at, straight, 0.0)
        return value if has is None else value * has

    sets = [(1, None, 2, None), (0, None, 3, None), (-3, has_left, -2, has_left), (5, has_right, 6, has_right), (-1, has_left, 4, has_right)]
    for i, (a, has_a, b, has_b) in enumerate(sets):
        high, middle = split2(jnp.concatenate([column(a, has_a), column(b, has_b)], axis=1))
        for j, part in enumerate((high, high, middle)):
            k_ref[:, (3 * i + j) * WIDE:(3 * i + j + 1) * WIDE] = part
    for d, (_, _, sent, _) in enumerate(dirs):
        shape = (16, 3 * WIDE)
        row, lane = iota(shape, 0), iota(shape, 1) & (WIDE - 1)
        pick = ((row >> 2) == (lane >> 6)) & ((row & 3) < R) & ((lane & 63) == sent + (row & 3))
        sel_ref[d] = one(pick).astype(BF16)
    for p, columns in enumerate(PARTS):
        for d, (_, has, _, got) in enumerate(dirs):
            shape = (2 * 256, 48)
            row, lane = iota(shape, 0), iota(shape, 1)
            side, slot = lane >> 4, lane & 15
            col = jnp.where((slot >> 3) == 0, columns[0], columns[1]) + 4 * (side - 1)
            out_c, out_r = row & 3, (row & 255) >> 2
            ok = ((slot & 3) < R) & (((slot >> 2) & 1) == (row >> 8))
            value = jnp.where(ok, -tap(out_r - got - (slot & 3)) * tap(out_c - col), 0.0)
            there = jnp.where(side == 0, has_left, jnp.where(side == 2, has_right, 1.0))
            value = value * there if has is None else value * there * one(has)
            high, middle = split2(value)
            for j, part in enumerate((high, high, middle)):
                tile_ref[d, :, (2 * j + p) * 48:(2 * j + p + 1) * 48] = part


def kernel(tile_rows, tiles, phases_ref, pairs_hbm, w_hbm, cls_hbm, out_ref,
           pairs_ref, w_ref, cls_ref, phase, blocks, recv, inc_ref, wpx_ref, lpx_ref, band, low, k_ref, sel_ref, tile_ref,
           z_ref, z_sent, z_got, theirs_ref, y_ref, x_ref, edge, halo_one, halo_two, halo_tile, acc,
           load_sem, own_sem, first_send, first_recv, near_send, near_recv, pair_send, pair_recv, send_sem, recv_sem):
    me, core = lax.axis_index("ifg"), lax.axis_index("tile")
    count = lax.axis_size("ifg")
    own = phase.shape[0]
    per = own // 2
    cols = phase.shape[2]
    left, right = lax.rem(me + count - 1, count), lax.rem(me + 1, count)
    has_left, has_right = me > 0, me < count - 1
    if tiles == 2:
        dirs = [(1 - core, None, jnp.where(core == 0, tile_rows - R, 0), jnp.where(core == 0, tile_rows, -R))]
    else:
        dirs = [(lax.rem(core + tiles - 1, tiles), core > 0, 0, -R),
                (lax.rem(core + 1, tiles), core < tiles - 1, tile_rows - R, tile_rows)]

    pieces = 4
    loads = []
    for i in range(pieces):
        for h in range(2):
            span = pl.ds(h * per + i * (per // pieces), per // pieces)
            loads.append(pltpu.make_async_copy(phases_ref.at[span], phase.at[span], load_sem.at[2 * i + h]))
            loads[-1].start()

    small = []
    for i, (src, dst) in enumerate(((pairs_hbm, pairs_ref), (w_hbm, w_ref), (cls_hbm, cls_ref))):
        small.append(pltpu.make_async_copy(src, dst, load_sem.at[8 + i]))
        small[-1].start()

    barrier = pltpu.get_barrier_semaphore()

    def greet(k, _):
        pl.semaphore_signal(barrier, inc=1, device_id=(lax.rem(me + k, count), core), device_id_type=MESH)
        return _

    lax.fori_loop(1, count, greet, 0)
    near = [[(me, tile), (left, tile), (right, tile)] for tile, _, _, _ in dirs]
    for group in near:
        for partner in group:
            pl.semaphore_signal(barrier, inc=1, device_id=partner, device_id_type=MESH)

    for i in range(pieces):
        loads[2 * i].wait()
        loads[2 * i + 1].wait()

        def turn(q, _):
            value = jnp.concatenate([phase[q], phase[q + per]], axis=0).T
            blocks[pl.ds(q, cols, stride=per), :] = value
            return _

        lax.fori_loop(i * (per // pieces), (i + 1) * (per // pieces), turn, 0, unroll=4)
    pl.semaphore_wait(barrier, count - 1 + 3 * len(dirs))

    half = count // 2
    base = jnp.where(me >= half, half, 0)
    away = half - base
    place = me - base
    partner = away + place

    def remote(src, dst, send, recv_at, device):
        return pltpu.make_async_remote_copy(src_ref=src, dst_ref=dst, send_sem=send, recv_sem=recv_at,
                                            device_id=(device, core), device_id_type=MESH)

    def block_of(owner, at, size):
        return blocks.at[pl.ds(pl.multiple_of(owner * 4 * per + at, 8), size)]

    def first_copy(j, far, src, c):
        start, i = (away, j) if far else (base, half + j)
        peer = start + lax.rem(place + j, half)
        return remote(block_of(peer, c * per, per), recv.at[src, pl.ds(c * per, per)], first_send.at[c - 1, i], first_recv.at[c - 1, i], peer)

    def near_copy(i, j, src):
        peer = lax.rem(place + j, half)
        at = 3 * per * (i % 2)
        owner, slot = (base + peer, base + src) if i < 2 else (away + peer, away + src)
        return remote(block_of(owner, at, per), recv.at[slot, pl.ds(at, per)], near_send.at[i, j], near_recv.at[i, j], base + peer)

    def each(begin, action):
        def body(j, _):
            action(j)
            return _

        lax.fori_loop(begin, half, body, 0)

    def source(j):
        return lax.rem(place + half - j, half)

    def near_start(kinds):
        def action(j):
            for i in kinds:
                near_copy(i, j, place).start()

        each(1, action)

    def near_wait(kinds):
        def action(j):
            for i in kinds:
                near_copy(i, j, source(j)).wait_recv()

        each(1, action)

    theirs = remote(cls_ref, theirs_ref, pair_send.at[2], pair_recv.at[2], partner)
    small[2].wait()
    theirs.start()
    each(1, lambda j: first_copy(j, False, me, 1).start())
    each(0, lambda j: first_copy(j, True, me, 1).start())
    near_start((2, 3))
    each(0, lambda j: first_copy(j, True, me, 2).start())
    each(1, lambda j: first_copy(j, False, me, 2).start())
    mine = [pltpu.make_async_copy(block_of(me, 0, 4 * per), recv.at[me], own_sem.at[0])]
    for i in range(2):
        at = 3 * per * i
        mine.append(pltpu.make_async_copy(block_of(partner, at, per), recv.at[partner, pl.ds(at, per)], own_sem.at[1 + i]))
    for c in mine:
        c.start()

    def absent(cond, *refs):
        @pl.when(jnp.logical_not(cond))
        def _():
            for ref in refs:
                ref[...] = jnp.zeros(ref.shape, F32)

    absent(has_left, halo_one.at[0], halo_two.at[0])
    absent(has_right, halo_one.at[1], halo_two.at[1])
    for p in range(2):
        for d, (_, has, _, _) in enumerate(dirs):
            absent(has_left if has is None else has_left & has, halo_tile.at[p, d, 0])
            absent(has_right if has is None else has_right & has, halo_tile.at[p, d, 2])
            if has is not None:
                absent(has, halo_tile.at[p, d, 1])

    for c in small[:2]:
        c.wait()
    prepare(pairs_ref, w_ref, cls_ref, theirs.wait_recv, theirs_ref, per, count, inc_ref, wpx_ref, lpx_ref, band, low)
    fill_filters(dirs, one(has_left), one(has_right), k_ref, sel_ref, tile_ref)
    for c in mine:
        c.wait()

    def take_first(c):
        each(0, lambda j: first_copy(j, True, away + source(j), c).wait_recv())
        each(1, lambda j: first_copy(j, False, base + source(j), c).wait_recv())

    low_lanes = iota((ROWS, LANES), 1) < LANES // 2

    def sums(values, left_sides):
        value = jnp.concatenate(split2(jnp.concatenate(values, axis=1)), axis=0)
        a, b = [dot_nn(side, value) for side in left_sides]
        packed = []
        for i in range(len(values)):
            at = slice(i * LANES, (i + 1) * LANES)
            aa, ab, ba, bb = a[:ROWS, at], a[ROWS:, at], b[:ROWS, at], b[ROWS:, at]
            packed.append(jnp.where(low_lanes, aa, bb) + swap(jnp.where(low_lanes, ab, ba)))
        return packed

    def first_side(c):
        value = recv[:, c * per:(c + 1) * per, :].reshape(count * per, LANES) * wpx_ref[c]
        z_ref[0:ROWS, :] = sums([value], [inc_ref[h] for h in range(2)])[0]

    def half_side(slots, weights):
        size = half * per
        span = pl.ds(pl.multiple_of(base * per, LANES), size)
        values = []
        for c, w in zip(PARTS[1], weights):
            got = recv[pl.ds(slots, half), c * per:(c + 1) * per, :].reshape(size, LANES)
            values.append(got * wpx_ref[w, span, :])
        sides = [inc_ref[h, :, span] for h in range(2)]
        return sums(values, [jnp.concatenate([side, side], axis=1) for side in sides])

    def forward(p):
        n = len(GROUPS[p])

        def step(t, a):
            at = pl.ds(t, n)
            y = a[0]
            y_ref[at, :] = y * lpx_ref[p, 0, at, :]
            return [v - lpx_ref[p, j + 1, at, :] * y for j, v in enumerate(a[1:])]

        def block(b, carry):
            a = list(carry)
            base = pl.multiple_of(b * 8 * n, 8 * n)
            for s in range(8):
                a = step(base + n * s, a + [z_ref[pl.ds(base + n * (s + 8), n), :]])
            return tuple(a)

        a = list(lax.fori_loop(0, BLOCKS, block, tuple(z_ref[n * t:n * t + n, :] for t in range(8))))
        for t in range(8 * BLOCKS, MEET):
            a = step(n * t, a + [z_ref[n * (t + 8):n * (t + 9), :]])
        a = [a[j] + swap(a[7 - j]) for j in range(8)]
        for t in range(MEET, LAST):
            a = step(n * t, a)

    def backward(p, send):
        n = len(GROUPS[p])
        refs = [x_ref.at[c] for c in GROUPS[p]]

        def step(t, later, keep=True):
            at = pl.ds(n * t, n)
            value = y_ref[at, :]
            for g in range(len(later), 0, -1):
                value = value - lpx_ref[p, g, at, :] * later[g - 1]
            if keep:
                for i, ref in enumerate(refs):
                    ref[pl.ds(t, 1), :] = value[i:i + 1]
            return [value] + later[:7]

        later = []
        for t in range(LAST - 1, 8 * BLOCKS - 1, -1):
            later = step(t, later, t < OUT)

        def block(b, carry):
            later = list(carry)
            base = pl.multiple_of(b * 8, 8)
            for s in range(7, -1, -1):
                later = step(base + s, later)
            return tuple(later)

        cut = CUT // 8
        carry = lax.fori_loop(0, BLOCKS - cut, lambda n, c: block(BLOCKS - 1 - n, c), tuple(later))
        send(0, pl.ds(CUT, OUT - CUT))
        lax.fori_loop(0, cut, lambda n, c: block(cut - 1 - n, c), carry)
        send(1, pl.ds(0, CUT))

    def copy(i, src, dst, device):
        return pltpu.make_async_remote_copy(src_ref=src, dst_ref=dst, send_sem=send_sem.at[i],
                                            recv_sem=recv_sem.at[i], device_id=device, device_id_type=MESH)

    sides = [[], []]

    def send_one(c):
        def send(piece, span):
            at = 4 * (c - 1) + 2 * piece
            src = x_ref.at[c, span]
            sides[0].append(copy(at, src, halo_one.at[1, c - 1, span], (left, core)))
            sides[1].append(copy(at + 1, src, halo_one.at[0, c - 1, span], (right, core)))
            pl.when(has_left)(sides[0][-1].start)
            pl.when(has_right)(sides[1][-1].start)

        return send

    def send_two(piece, span):
        sides[0].append(copy(8 + 2 * piece, x_ref.at[0, span], halo_two.at[1, span], (left, core)))
        sides[1].append(copy(9 + 2 * piece, x_ref.at[3, span], halo_two.at[0, span], (right, core)))
        pl.when(has_left)(sides[0][-1].start)
        pl.when(has_right)(sides[1][-1].start)

    edges = []

    def both(a, b):
        return b if a is None else a if b is None else a & b

    def when(cond, action):
        action() if cond is None else pl.when(cond)(action)

    def solved(p):
        value = jnp.concatenate([x_ref[c] for c in PARTS[p]], axis=1)
        return split3(value)

    def send_edges(p, parts):
        for d, (_, has, _, _) in enumerate(dirs):
            edge[p, d] = dot_nt(sel_ref[d], jnp.concatenate(parts, axis=1))
            opposite = len(dirs) - 1 - d
            got = dirs[opposite][1]
            for i, (slot, to, came) in enumerate(((1, None, None), (2, has_left, has_right), (0, has_right, has_left))):
                c = copy(12 + (p * len(dirs) + d) * 3 + i, edge.at[p, d], halo_tile.at[p, opposite, slot], near[d][i])
                edges.append((c, both(has, to), both(got, came)))
                when(edges[-1][1], c.start)

    def apply(i, *values):
        wide = [v for high, middle, *_ in values for v in (high, middle, high)]
        return dot_nt(k_ref[:, 3 * WIDE * i:3 * WIDE * (i + len(values))], jnp.concatenate(wide, axis=1))

    def apply_tile():
        total = None
        for d in range(len(dirs)):
            pair = [split2(halo_tile[p, d].reshape(48, OUT)) for p in range(2)]
            order = [pair[0][0], pair[1][0], pair[0][1], pair[1][1], pair[0][0], pair[1][0]]
            term = dot_nn(tile_ref[d], jnp.concatenate(order, axis=0))
            total = term if total is None else total + term
        return total

    def wait_sides(begin, end):
        for i in range(begin, end):
            pl.when(has_right)(sides[0][i].wait_recv)
            pl.when(has_left)(sides[1][i].wait_recv)

    take_first(1)
    first_side(1)
    forward(0)
    backward(0, send_one(1))
    near_wait((2, 3))
    for i, z in enumerate(half_side(away, (4, 5))):
        z_sent[i] = z[:OUT]
    summed = [remote(z_sent.at[i], z_got.at[i], pair_send.at[i], pair_recv.at[i], partner) for i in range(2)]
    for c in summed:
        c.start()
    near_start((0, 1))
    take_first(2)
    first_side(2)
    forward(1)
    backward(1, send_one(2))
    parts = solved(0)
    send_edges(0, parts)
    acc[...] = apply(0, parts)

    near_wait((0, 1))
    nearby = half_side(base, PARTS[1])
    for i, z in enumerate(nearby):
        summed[i].wait_recv()
        z_ref[pl.ds(i, OUT, stride=2), :] = z[:OUT] + z_got[i]
        z_ref[pl.ds(2 * OUT + i, ROWS - OUT, stride=2), :] = z[OUT:]
    forward(2)
    backward(2, send_two)
    parts = solved(1)
    send_edges(1, parts)
    acc[...] += apply(1, parts)
    wait_sides(0, 4)
    for c, _, came in edges[:3 * len(dirs)]:
        when(came, c.wait_recv)
    beside = [split2(jnp.concatenate([halo_one[side, 0], halo_one[side, 1]], axis=1)) for side in range(2)]
    total = acc[...] + apply(2, *beside)
    for c, _, came in edges[3 * len(dirs):]:
        when(came, c.wait_recv)
    total += apply_tile()
    wait_sides(4, 6)
    total += apply(4, split2(jnp.concatenate([halo_two[0], halo_two[1]], axis=1)))

    front, back = total[:256], split2(total[256:])
    row, lane = iota((OUT, DATES), 0), iota((OUT, DATES), 1)
    turned = one((row < HALF) & (row == DATES - 1 - lane)).astype(BF16)
    later = dot_nn(back[0], turned) + dot_nn(back[1], turned)
    tail = jnp.where(iota((256, OUT - LANES), 1) < HALF - LANES, front[:, LANES:OUT], 0.0)
    first, second = front[:, 0:LANES], later[:, LANES:OUT] + tail
    for r in range(tile_rows):
        at = slice(4 * r, 4 * r + 4)
        out_ref[r, :, 0:LANES] = first[at]
        out_ref[r, :, LANES:DATES] = later[at, LANES:]
        out_ref[r, :, LANES:OUT] = second[at]

    def sent(j, far):
        for c in PARTS[0]:
            first_copy(j, far, me, c).wait_send()
        if not far:
            for i in range(4):
                near_copy(i, j, place).wait_send()

    each(0, functools.partial(sent, far=True))
    each(1, functools.partial(sent, far=False))
    for c in [theirs] + summed:
        c.wait_send()
    for has, group in ((has_left, sides[0]), (has_right, sides[1])):
        for c in group:
            pl.when(has)(c.wait_send)
    for c, went, _ in edges:
        when(went, c.wait_send)


def on_device(tiles, phases, pairs, class_weights, classes):
    own, tile_rows, cols = phases.shape
    tile_cols = classes.shape[1]
    count = cols // tile_cols
    assert tile_rows == 64 and tile_cols == 4 and count % 2 == 0
    if own % 16:
        more = -own % 16
        phases = jnp.pad(phases, ((0, more), (0, 0), (0, 0)))
        pairs = jnp.pad(pairs.reshape(count, own, 2), ((0, 0), (0, more), (0, 0))).reshape(-1, 2)
        class_weights = jnp.pad(class_weights.reshape(CLASSES, count, own), ((0, 0), (0, 0), (0, more))).reshape(CLASSES, -1)
        own += more
    nifg = pairs.shape[0]
    per = own // 2
    dirs = 1 if tiles == 2 else 2
    vmem = pl.BlockSpec(memory_space=pltpu.VMEM)
    copies = 12 + 6 * dirs

    corrected = pl.pallas_call(
        functools.partial(kernel, tile_rows, tiles),
        out_shape=jax.ShapeDtypeStruct((tile_rows, tile_cols, DATES), F32),
        in_specs=[pl.BlockSpec(memory_space=pltpu.HBM)] * 4,
        out_specs=vmem,
        scratch_shapes=[
            pltpu.VMEM((2, nifg), jnp.int32),
            pltpu.VMEM((CLASSES, nifg), F32),
            pltpu.VMEM((tile_cols, tile_rows), jnp.int32),
            pltpu.VMEM((own, tile_rows, cols), F32),
            pltpu.VMEM((cols * per, LANES), F32),
            pltpu.VMEM((count, 4 * per, LANES), F32),
            pltpu.VMEM((2, 2 * ROWS, nifg), BF16),
            pltpu.VMEM((6, nifg // 2, LANES), F32),
            pltpu.VMEM((3, MAXGAP + 1, 2 * ROWS, LANES), F32),
            pltpu.VMEM((MAXGAP + 1, ROWS, LANES), F32),
            pltpu.VMEM((MAXGAP + 1, ROWS, LANES), F32),
            pltpu.VMEM((2 * 256, 15 * WIDE), BF16),
            pltpu.VMEM((dirs, 16, 3 * WIDE), BF16),
            pltpu.VMEM((dirs, 2 * 256, 6 * 48), BF16),
            pltpu.VMEM((2 * ROWS, LANES), F32),
            pltpu.VMEM((2, OUT, LANES), F32),
            pltpu.VMEM((2, OUT, LANES), F32),
            pltpu.VMEM((tile_cols, tile_rows), jnp.int32),
            pltpu.VMEM((2 * ROWS, LANES), F32),
            pltpu.VMEM((4, OUT, LANES), F32),
            pltpu.VMEM((2, dirs, 16, OUT), F32),
            pltpu.VMEM((2, 2, OUT, LANES), F32),
            pltpu.VMEM((2, OUT, LANES), F32),
            pltpu.VMEM((2, dirs, 3, 16, OUT), F32),
            pltpu.VMEM((2 * 256, OUT), F32),
            pltpu.SemaphoreType.DMA((11,)),
            pltpu.SemaphoreType.DMA((3,)),
            pltpu.SemaphoreType.DMA((2, count)),
            pltpu.SemaphoreType.DMA((2, count)),
            pltpu.SemaphoreType.DMA((4, count // 2)),
            pltpu.SemaphoreType.DMA((4, count // 2)),
            pltpu.SemaphoreType.DMA((3,)),
            pltpu.SemaphoreType.DMA((3,)),
            pltpu.SemaphoreType.DMA((copies,)),
            pltpu.SemaphoreType.DMA((copies,)),
        ],
        compiler_params=pltpu.CompilerParams(
            collective_id=0, has_side_effects=True, vmem_limit_bytes=58 * 1024 * 1024
        ),
        name="invert_and_filter",
    )(phases, pairs.T, class_weights, classes.T)
    return corrected


def solution(mesh):
    return jax.shard_map(
        functools.partial(on_device, mesh.shape["tile"]),
        mesh=mesh,
        in_specs=(P("ifg", "tile", None), P(), P(), P("tile", "ifg")),
        out_specs=P("tile", "ifg", None),
        check_vma=False,
    )
```
